32 devices in a mesh: seq: 16 (over z, y, core), head: 2 (over x).
Axes of the slice: x: 2, y: 2, z: 4, core: 2. Of those that a mesh axis runs over, the one named last changes fastest.
Arguments:
- tokens: bfloat16 [2, 64, 4096], P(None, None, 'seq'), may hold values from -6 to 6
- lengths: int32 [64], replicated, may hold values from 1 to 8192, as said below
- page_owner: int32 [512], P('seq'), may hold values from -1 to 63, as said below
- page_number: int32 [512], P('seq'), may hold values from 0 to 127, as said below
- key_pages: bfloat16 [512, 64, 4096], P('seq', None, 'head'), may hold values from -600 to 600
- value_pages: bfloat16 [512, 64, 4096], P('seq', None, 'head'), may hold values from -6 to 6
- alibi_slopes: float32 [32], P('head'), as said below
- norm1_gain: float32 [4096], P('seq'), may hold values from 0.1 to 1.9
- norm2_gain: float32 [4096], P('seq'), may hold values from 0.1 to 1.9
- w_qkv: bfloat16 [4096, 3, 4096], P('seq', None, 'head'), may hold values from -0.09375 to 0.09375
- w_out: bfloat16 [4096, 4096], P('seq', 'head'), may hold values from -0.09375 to 0.09375
- w_up: bfloat16 [4096, 16384], P('seq', 'head'), may hold values from -0.09375 to 0.09375
- w_down: bfloat16 [4096, 16384], P('seq', 'head'), may hold values from -0.046875 to 0.046875
Outputs:
- layer_out: bfloat16 [2, 64, 4096], P(None, None, 'seq')
The draws below stay inside these ranges and needn't reach their ends.
Inputs may be any that keep to these rules, and one draw needn't show every extreme that they name: Exactly one request holds 8192 tokens; request r's cache fills page_number 0 .. ceil(lengths[r] / 64) - 1. `page_owner`: -1 marks a free slot; every page of every request stands in exactly one slot; on some indices of seq all 32 slots are used. `page_number`: 0 for free slots. `alibi_slopes`: Positive.
All inputs are finite; a program needn't handle non-finite values.
Results may differ from the reference program's by a relative error of at most 0.011.
Values may be sent and summed in bfloat16 or wider, within the bound.
A program may use at most 128 MiB of HBM per device.

```python
import math
import jax
import jax.numpy as jnp
from jax import lax

D = 4096
NH = 32
HD = 128
FF = 16384
REQ = 64
STEPS = 2
PAGE = 64
PAGES_DEV = 32
BLK = 8
POOL = 512
MAXLEN = 8192
SPREAD = 1


def page_table(base_key):
    split_keys = jax.random.split(jax.random.fold_in(base_key, 7), 6)
    longest_pages = MAXLEN // PAGE
    seq_count = POOL // PAGES_DEV
    half_count = seq_count // 2
    request_ids = jnp.arange(REQ, dtype=jnp.int32)
    extra_pages = jax.random.randint(split_keys[0], (REQ,), 0, 2 * SPREAD)
    long_request = jax.random.randint(split_keys[1], (), 0, REQ)
    page_counts = jnp.where(request_ids == long_request, longest_pages, 1 + extra_pages).astype(jnp.int32)
    tail_tokens = jax.random.randint(split_keys[2], (REQ,), 1, PAGE + 1)
    tail_tokens = jnp.where(request_ids == long_request, PAGE, tail_tokens)
    lengths = ((page_counts - 1) * PAGE + tail_tokens).astype(jnp.int32)
    page_ends = jnp.cumsum(page_counts).astype(jnp.int32)
    page_starts = page_ends - page_counts
    global_page = jnp.arange(POOL, dtype=jnp.int32)
    owner_list = jnp.sum((global_page[:, None] >= page_ends[None, :]).astype(jnp.int32), axis=1)
    live_page = global_page < page_ends[REQ - 1]
    safe_list = jnp.clip(owner_list, 0, REQ - 1)
    number_list = global_page - jnp.take(page_starts, safe_list)
    owner_list = jnp.where(live_page, safe_list, -1).astype(jnp.int32)
    number_list = jnp.where(live_page, number_list, 0).astype(jnp.int32)
    pair_order = jax.random.permutation(split_keys[3], half_count)
    heavy_pair = pair_order < max(1, seq_count // 4)
    heavy_side = jax.random.randint(split_keys[4], (half_count,), 0, 2)
    device_ids = jnp.arange(seq_count, dtype=jnp.int32)
    pair_index = device_ids % half_count
    upper_side = (device_ids >= half_count).astype(jnp.int32)
    heavy_device = jnp.take(heavy_pair, pair_index) & (jnp.take(heavy_side, pair_index) == upper_side)
    capacity = jnp.where(heavy_device, PAGES_DEV, PAGES_DEV // 2)
    slot_ids = jnp.arange(POOL, dtype=jnp.int32)
    allowed = slot_ids % PAGES_DEV < jnp.take(capacity, slot_ids // PAGES_DEV)
    heavy_slot = jnp.take(heavy_device, slot_ids // PAGES_DEV)
    slot_rank = jax.random.permutation(split_keys[5], POOL).astype(jnp.int32)
    order_key = jnp.where(allowed, jnp.where(heavy_slot, 0, POOL), 2 * POOL) + slot_rank
    slot_order = jnp.argsort(order_key)
    owners = jnp.full((POOL,), -1, jnp.int32).at[slot_order].set(owner_list)
    numbers = jnp.zeros((POOL,), jnp.int32).at[slot_order].set(number_list)
    return (lengths, owners, numbers)


def draw_lengths(key, part):
    return page_table(key)[0]


def draw_page_owner(key, part):
    return page_table(key)[1]


def draw_page_number(key, part):
    return page_table(key)[2]


def draw_key_pages(key, part):
    split_keys = jax.random.split(jax.random.fold_in(key, 11), 1)
    base_values = jax.random.truncated_normal(split_keys[0], -6.0, 6.0, (POOL, PAGE, D), jnp.float32)
    return base_values.astype(jnp.bfloat16)


def draw_alibi_slopes(key, part):
    split_keys = jax.random.split(jax.random.fold_in(key, 13), 3)
    slow_share = 0.5
    slow_head = jax.random.uniform(split_keys[0], (NH,), jnp.float32) < slow_share
    slow_rate = jnp.exp(jax.random.uniform(split_keys[1], (NH,), jnp.float32, math.log(0.2), math.log(2.0))) / MAXLEN
    fast_rate = jnp.exp(jax.random.uniform(split_keys[2], (NH,), jnp.float32, math.log(1.0 / 50.0), math.log(1.0 / 30.0)))
    return jnp.where(slow_head, slow_rate, fast_rate).astype(jnp.float32)


def block_scale(key, shape, pieces, smallest, largest):
    loudness = 1.0
    for position, blocks in pieces:
        heights = jax.random.uniform(jax.random.fold_in(jax.random.fold_in(key, 6), position), (blocks,), jnp.float32, smallest / len(pieces), largest / len(pieces))
        loudness = loudness * jnp.repeat(jnp.exp(heights), shape[position] // blocks).reshape((-1,) + (1,) * (len(shape) - 1 - position))
    return loudness


def noise(stream_key, shape, spread, bound, pieces=(), held_as=jnp.bfloat16):
    drawn = spread * jax.random.normal(stream_key, shape, jnp.float32)
    if pieces:
        drawn = drawn * block_scale(stream_key, shape, pieces, -0.22, 0.18)
    return jnp.clip(drawn, -bound, bound).astype(held_as)


def setup_inputs(seed: int = 0) -> dict:
    keys = jax.random.split(jax.random.key(seed), 14)
    tokens = noise(keys[0], (STEPS, REQ, D), 1.0, 6.0, ((2, 16),))
    lengths = draw_lengths(jax.random.fold_in(keys[13], 71), 0)
    page_owner = draw_page_owner(jax.random.fold_in(keys[13], 71), 0)
    page_number = draw_page_number(jax.random.fold_in(keys[13], 71), 0)
    key_pages = draw_key_pages(jax.random.fold_in(keys[13], 71), 0)
    value_pages = noise(keys[5], (POOL, PAGE, D), 1.0, 6.0, ((0, 16), (2, 2)))
    alibi_slopes = draw_alibi_slopes(jax.random.fold_in(keys[13], 71), 0)
    norm1_gain = jnp.clip(1.0 + 0.18 * jax.random.normal(keys[7], (D,), jnp.float32), 0.1, 1.9)
    norm2_gain = jnp.clip(1.0 + 0.18 * jax.random.normal(keys[8], (D,), jnp.float32), 0.1, 1.9)
    w_qkv = noise(keys[9], (D, 3, D), D ** -0.5, 0.09375, ((0, 16), (2, 2)))
    w_out = noise(keys[10], (D, D), D ** -0.5, 0.09375, ((0, 16), (1, 2)))
    w_up = noise(keys[11], (D, FF), D ** -0.5, 0.09375, ((0, 16), (1, 2)))
    w_down = noise(keys[12], (D, FF), FF ** -0.5, 0.046875, ((0, 16), (1, 2)))
    return {"tokens": tokens, "lengths": lengths, "page_owner": page_owner, "page_number": page_number, "key_pages": key_pages, "value_pages": value_pages, "alibi_slopes": alibi_slopes, "norm1_gain": norm1_gain, "norm2_gain": norm2_gain, "w_qkv": w_qkv, "w_out": w_out, "w_up": w_up, "w_down": w_down}


eps_norm = 1e-05
floor_score = -1e+30
highest = lax.Precision.HIGHEST

def normalize(token_rows, gain_full, width_all):
    token_float = token_rows.astype(jnp.float32)
    mean_value = lax.optimization_barrier(jnp.sum(token_float, axis=1)) / width_all
    variance = lax.optimization_barrier(jnp.sum(token_float * token_float, axis=1)) / width_all - mean_value * mean_value
    return ((token_float - mean_value[:, None]) * lax.rsqrt(variance + eps_norm)[:, None] * gain_full[None, :]).astype(jnp.bfloat16)

def page_block(carry_state, owners, number, key_block, value_block, queries, slopes, lengths, token_step):
    run_max, run_sum, run_out = carry_state
    nblock, page_len, width_all = key_block.shape
    nheads = slopes.shape[0]
    head_size = width_all // nheads
    requests = queries.shape[0]
    safe_owner = jnp.clip(owners, 0, requests - 1)
    page_query = jnp.take(queries, safe_owner, axis=0).astype(jnp.float32)
    key_heads = key_block.reshape(nblock, page_len, nheads, head_size).astype(jnp.float32)
    value_heads = value_block.reshape(nblock, page_len, nheads, head_size).astype(jnp.float32)
    scores = jnp.einsum('bhe,bthe->bth', page_query, key_heads) * head_size ** (-0.5)
    positions = number[:, None] * page_len + jnp.arange(page_len, dtype=jnp.int32)[None, :]
    own_length = jnp.take(lengths, safe_owner)
    distance = (own_length[:, None] + token_step - positions).astype(jnp.float32)
    scores = scores - distance[:, :, None] * slopes[None, None, :]
    valid_mask = (owners[:, None] >= 0) & (positions < own_length[:, None])
    masked = jnp.where(valid_mask[:, :, None], scores, floor_score)
    page_max = lax.optimization_barrier(jnp.max(masked, axis=1))
    member = owners[None, :] == jnp.arange(requests, dtype=jnp.int32)[:, None]
    block_max = lax.optimization_barrier(jnp.max(jnp.where(member[:, :, None], page_max[None, :, :], floor_score), axis=1))
    next_max = jnp.maximum(run_max, block_max)
    owner_max = jnp.take(next_max, safe_owner, axis=0)
    expon = jnp.where(valid_mask[:, :, None], jnp.exp(masked - owner_max[:, None, :]), 0.0)
    page_sum = lax.optimization_barrier(jnp.sum(expon, axis=1))
    weights = lax.optimization_barrier(expon.astype(jnp.bfloat16)).astype(jnp.float32)
    page_out = jnp.einsum('bth,bthe->bhe', weights, value_heads)
    member_float = member.astype(jnp.float32)
    rescale = jnp.exp(run_max - next_max)
    next_sum = run_sum * rescale + jnp.dot(member_float, page_sum, precision=highest)
    added = jnp.dot(member_float, page_out.reshape(nblock, nheads * head_size), precision=highest)
    next_out = run_out * rescale[:, :, None] + added.reshape(requests, nheads, head_size)
    return (next_max, next_sum, next_out)

def attend_new(carry_state, queries, new_keys, new_values, slopes, token_step):
    run_max, run_sum, run_out = carry_state
    head_size = queries.shape[2]
    for earlier in range(token_step + 1):
        scores = lax.optimization_barrier(jnp.sum(queries.astype(jnp.float32) * new_keys[earlier].astype(jnp.float32), axis=2)) * head_size ** (-0.5)
        scores = scores - slopes[None, :] * float(token_step - earlier)
        next_max = jnp.maximum(run_max, scores)
        rescale = jnp.exp(run_max - next_max)
        expon = jnp.exp(scores - next_max)
        weights = lax.optimization_barrier(expon.astype(jnp.bfloat16)).astype(jnp.float32)
        run_sum = run_sum * rescale + expon
        run_out = run_out * rescale[:, :, None] + weights[:, :, None] * new_values[earlier].astype(jnp.float32)
        run_max = next_max
    attended = (run_out / run_sum[:, :, None]).astype(jnp.bfloat16)
    return attended.reshape(attended.shape[0], -1)

def reference(tokens, lengths, page_owner, page_number, key_pages, value_pages, alibi_slopes, norm1_gain, norm2_gain, w_qkv, w_out, w_up, w_down):
    requests = tokens.shape[1]
    nblocks = POOL // BLK
    owner_blocks = page_owner.reshape(nblocks, BLK)
    number_blocks = page_number.reshape(nblocks, BLK)
    key_blocks = key_pages.reshape(nblocks, BLK, PAGE, D)
    value_blocks = value_pages.reshape(nblocks, BLK, PAGE, D)
    new_keys = []
    new_values = []
    outputs = []
    for token_step in range(STEPS):
        token_rows = tokens[token_step]
        token_float = token_rows.astype(jnp.float32)
        normed = normalize(token_rows, norm1_gain, D)
        joined = jnp.dot(normed, w_qkv.reshape(D, 3 * D), preferred_element_type=jnp.float32).astype(jnp.bfloat16)
        queries = joined[:, :D].reshape(requests, NH, HD)
        new_keys.append(joined[:, D:2 * D].reshape(requests, NH, HD))
        new_values.append(joined[:, 2 * D:].reshape(requests, NH, HD))
        initial = (jnp.full((requests, NH), floor_score, jnp.float32), jnp.zeros((requests, NH), jnp.float32), jnp.zeros((requests, NH, HD), jnp.float32))

        def page_step(carry_state, block_items):
            owners, number, key_block, value_block = block_items
            return (page_block(carry_state, owners, number, key_block, value_block, queries, alibi_slopes, lengths, token_step), None)
        final_state, _ = lax.scan(page_step, initial, (owner_blocks, number_blocks, key_blocks, value_blocks))
        attended = attend_new(final_state, queries, new_keys, new_values, alibi_slopes, token_step)
        projected = lax.dot_general(attended, w_out, (((1,), (1,)), ((), ())), preferred_element_type=jnp.float32)
        hidden_in = (token_float + projected).astype(jnp.bfloat16)
        hidden_float = hidden_in.astype(jnp.float32)
        normed_two = normalize(hidden_in, norm2_gain, D)
        up_proj = jnp.dot(normed_two, w_up, preferred_element_type=jnp.float32)
        hidden = jax.nn.gelu(up_proj, approximate=False).astype(jnp.bfloat16)
        down_proj = lax.dot_general(hidden, w_down, (((1,), (1,)), ((), ())), preferred_element_type=jnp.float32)
        outputs.append((hidden_float + down_proj).astype(jnp.bfloat16))
    return jnp.stack(outputs)
```

```python
import functools

import jax
import jax.numpy as jnp
from jax import lax
from jax.experimental import pallas as pl
from jax.experimental.pallas import tpu as pltpu
from jax.sharding import PartitionSpec as P

D = 4096
BLK = 8


eps_norm = 1e-05
floor_score = -1e30
highest = lax.Precision.HIGHEST


def normalize(token_rows, gain_share, totals, width_all):
    row_sum, row_squares = totals
    mean_value = row_sum / width_all
    variance = row_squares / width_all - mean_value * mean_value
    return (
        (token_rows.astype(jnp.float32) - mean_value[:, None])
        * lax.rsqrt(variance + eps_norm)[:, None]
        * gain_share[None, :]
    ).astype(jnp.bfloat16)


def page_block(
    carry_state, owners, number, key_block, value_block, queries, slopes, lengths, token_step
):
    run_max, run_sum, run_out = carry_state
    nblock, page_len, width_all = key_block.shape
    nheads = slopes.shape[0]
    head_size = width_all // nheads
    requests = queries.shape[0]
    safe_owner = jnp.clip(owners, 0, requests - 1)
    page_query = jnp.take(queries, safe_owner, axis=0)
    key_heads = key_block.reshape(nblock, page_len, nheads, head_size)
    value_heads = value_block.reshape(nblock, page_len, nheads, head_size)
    scores = jnp.einsum(
        "bhe,bthe->bth", page_query, key_heads, preferred_element_type=jnp.float32
    ) * head_size ** (-0.5)
    positions = number[:, None] * page_len + jnp.arange(page_len, dtype=jnp.int32)[None, :]
    own_length = jnp.take(lengths, safe_owner)
    distance = (own_length[:, None] + token_step - positions).astype(jnp.float32)
    scores = scores - distance[:, :, None] * slopes[None, None, :]
    valid_mask = (owners[:, None] >= 0) & (positions < own_length[:, None])
    masked = jnp.where(valid_mask[:, :, None], scores, floor_score)
    page_max = jnp.max(masked, axis=1)
    member = owners[None, :] == jnp.arange(requests, dtype=jnp.int32)[:, None]
    block_max = jnp.max(jnp.where(member[:, :, None], page_max[None, :, :], floor_score), axis=1)
    next_max = jnp.maximum(run_max, block_max)
    owner_max = jnp.take(next_max, safe_owner, axis=0)
    expon = jnp.where(valid_mask[:, :, None], jnp.exp(masked - owner_max[:, None, :]), 0.0)
    page_sum = jnp.sum(expon, axis=1)
    weights = expon.astype(jnp.bfloat16)
    page_out = jnp.einsum("bth,bthe->bhe", weights, value_heads, preferred_element_type=jnp.float32)
    member_float = member.astype(jnp.float32)
    rescale = jnp.exp(run_max - next_max)
    next_sum = run_sum * rescale + jnp.dot(member_float, page_sum, precision=highest)
    added = jnp.dot(member_float, page_out.reshape(nblock, nheads * head_size), precision=highest)
    next_out = run_out * rescale[:, :, None] + added.reshape(requests, nheads, head_size)
    return (next_max, next_sum, next_out)


def attend_new(carry_state, queries, new_keys, new_values, slopes, token_step):
    run_max, run_sum, run_out = carry_state
    head_size = queries.shape[2]
    for earlier in range(token_step + 1):
        scores = jnp.sum(
            queries.astype(jnp.float32) * new_keys[earlier].astype(jnp.float32), axis=2
        ) * head_size ** (-0.5)
        scores = scores - slopes[None, :] * float(token_step - earlier)
        next_max = jnp.maximum(run_max, scores)
        rescale = jnp.exp(run_max - next_max)
        expon = jnp.exp(scores - next_max)
        weights = lax.optimization_barrier(expon.astype(jnp.bfloat16)).astype(jnp.float32)
        run_sum = run_sum * rescale + expon
        run_out = run_out * rescale[:, :, None] + weights[:, :, None] * new_values[earlier].astype(
            jnp.float32
        )
        run_max = next_max
    attended = (run_out / run_sum[:, :, None]).astype(jnp.bfloat16)
    return attended.reshape(attended.shape[0], -1)


def on_device(
    tokens,
    lengths,
    page_owner,
    page_number,
    key_pages,
    value_pages,
    alibi_slopes,
    norm1_gain,
    norm2_gain,
    w_qkv,
    w_out,
    w_up,
    w_down,
):
    nsteps, requests, local_width = tokens.shape
    nheads = alibi_slopes.shape[0]
    head_width = key_pages.shape[2]
    head_size = head_width // nheads
    nblocks = key_pages.shape[0] // BLK
    qkv_width = w_qkv.shape[1] * w_qkv.shape[2]
    new_keys = []
    new_values = []
    outputs = []
    for token_step in range(nsteps):
        token_rows = tokens[token_step]
        token_float = token_rows.astype(jnp.float32)
        totals = lax.psum(
            (jnp.sum(token_float, axis=1), jnp.sum(token_float * token_float, axis=1)), "seq"
        )
        normed = normalize(token_rows, norm1_gain, totals, D)
        partial_qkv = jnp.dot(
            normed, w_qkv.reshape(local_width, qkv_width), preferred_element_type=jnp.float32
        )
        joined = lax.psum(partial_qkv, "seq").astype(jnp.bfloat16)
        queries = joined[:, :head_width].reshape(requests, nheads, head_size)
        new_keys.append(joined[:, head_width : 2 * head_width].reshape(requests, nheads, head_size))
        new_values.append(joined[:, 2 * head_width :].reshape(requests, nheads, head_size))
        carry_state = (
            jnp.full((requests, nheads), floor_score, jnp.float32),
            jnp.zeros((requests, nheads), jnp.float32),
            jnp.zeros((requests, nheads, head_size), jnp.float32),
        )

        def visit(turn_index, state_in):
            first_page = (turn_index * BLK).astype(jnp.int32)
            owners = lax.dynamic_slice_in_dim(page_owner, first_page, BLK, 0)
            number = lax.dynamic_slice_in_dim(page_number, first_page, BLK, 0)
            key_block = lax.dynamic_slice_in_dim(key_pages, first_page, BLK, 0)
            value_block = lax.dynamic_slice_in_dim(value_pages, first_page, BLK, 0)

            def compute(state_given):
                return page_block(
                    state_given,
                    owners,
                    number,
                    key_block,
                    value_block,
                    queries,
                    alibi_slopes,
                    lengths,
                    token_step,
                )

            def keep_state(state_given):
                return state_given

            return lax.cond(jnp.any(owners >= 0), compute, keep_state, state_in)

        carry_state = lax.fori_loop(0, nblocks, visit, carry_state)
        run_max, run_sum, run_out = carry_state
        top_max = lax.pmax(run_max, "seq")
        rescale = jnp.exp(run_max - top_max)
        run_sum, run_out = lax.psum((run_sum * rescale, run_out * rescale[:, :, None]), "seq")
        run_max = top_max
        attended = attend_new(
            (run_max, run_sum, run_out), queries, new_keys, new_values, alibi_slopes, token_step
        )
        projected = lax.psum(
            lax.dot_general(
                attended, w_out, (((1,), (1,)), ((), ())), preferred_element_type=jnp.float32
            ),
            "head",
        )
        hidden_in = (token_float + projected).astype(jnp.bfloat16)
        hidden_float = hidden_in.astype(jnp.float32)
        totals_two = lax.psum(
            (jnp.sum(hidden_float, axis=1), jnp.sum(hidden_float * hidden_float, axis=1)), "seq"
        )
        normed_two = normalize(hidden_in, norm2_gain, totals_two, D)
        up_proj = jnp.dot(normed_two, w_up, preferred_element_type=jnp.float32)
        up_share = lax.psum_scatter(up_proj, "seq", scatter_dimension=1, tiled=True)
        hidden_share = jax.nn.gelu(up_share, approximate=False).astype(jnp.bfloat16)
        down_part = lax.dot_general(
            lax.all_gather(hidden_share, "seq", axis=1, tiled=True),
            w_down,
            (((1,), (1,)), ((), ())),
            preferred_element_type=jnp.float32,
        )
        down_proj = lax.psum(down_part, "head")
        outputs.append((hidden_float + down_proj).astype(jnp.bfloat16))
    return jnp.stack(outputs)

MESH = pl.DeviceIdType.MESH
NSEQ = 16
NZ = 4
CHUNKS = 2
VMEM_LIMIT = 60 * 1024 * 1024


def place():
    index = lax.axis_index("seq")
    return index, index // 4, (index // 2) % 2, index % 2


def send(src, dst, send_sem, recv_sem, peer, axis="seq"):
    copy = pltpu.make_async_remote_copy(
        src_ref=src,
        dst_ref=dst,
        send_sem=send_sem,
        recv_sem=recv_sem,
        device_id={axis: peer},
        device_id_type=MESH,
    )
    copy.start()
    return copy


def greet_all(with_head):
    me = lax.axis_index("seq")
    barrier = pltpu.get_barrier_semaphore()
    for step in range(1, NSEQ):
        pl.semaphore_signal(
            barrier, inc=1, device_id={"seq": (me + step) % NSEQ}, device_id_type=MESH
        )
    if with_head:
        other = 1 - lax.axis_index("head")
        pl.semaphore_signal(barrier, inc=1, device_id={"head": other}, device_id_type=MESH)
    pl.semaphore_wait(barrier, NSEQ - 1 + int(with_head))


def row_to_column(row):
    width = row.shape[1]
    same = lax.broadcasted_iota(jnp.int32, (width, width), 0) == lax.broadcasted_iota(
        jnp.int32, (width, width), 1
    )
    return jnp.sum(jnp.where(same, row, 0.0), axis=1, keepdims=True)


def start_stats(values, stats, send_sem, recv_sem):
    me = lax.axis_index("seq")
    ones = jnp.ones((8, values.shape[1]), jnp.float32)
    contract = (((1,), (1,)), ((), ()))
    stats[me, 0:8, :] = lax.dot_general(
        ones, values, contract, precision=highest, preferred_element_type=jnp.float32
    )
    stats[me, 8:16, :] = lax.dot_general(
        ones, values * values, contract, precision=highest, preferred_element_type=jnp.float32
    )
    return [
        send(
            stats.at[me],
            stats.at[me],
            send_sem.at[step - 1],
            recv_sem.at[step - 1],
            (me + step) % NSEQ,
        )
        for step in range(1, NSEQ)
    ]


def finish_stats(copies, stats):
    for copy in copies:
        copy.wait_recv()
    total = stats[0]
    for source in range(1, NSEQ):
        total = total + stats[source]
    mean = total[0:1, :] / D
    variance = total[8:9, :] / D - mean * mean
    return row_to_column(mean), row_to_column(lax.rsqrt(variance + eps_norm))


def row_chunks(rows):
    size = rows // CHUNKS
    return [pl.ds(k * size, size) for k in range(CHUNKS)]


def add_into(target, extra):
    target[...] = (target[...].astype(jnp.float32) + extra[...].astype(jnp.float32)).astype(
        jnp.bfloat16
    )


def reduce_scatter(parts, from_core, from_y, from_z, send_sem, recv_sem, finish):
    me, z, y, c = place()
    chunks = row_chunks(parts.shape[3])
    copies = []
    first = []
    for k, rows in enumerate(chunks):
        sem = 5 * k
        first.append(
            send(
                parts.at[1 - c, :, :, rows],
                from_core.at[:, :, rows],
                send_sem.at[sem],
                recv_sem.at[sem],
                me + 1 - 2 * c,
            )
        )
    second = []
    for k, rows in enumerate(chunks):
        first[k].wait_recv()
        for zz in range(NZ):
            add_into(parts.at[c, 1 - y, zz, rows], from_core.at[1 - y, zz, rows])
        sem = 5 * k + 1
        second.append(
            send(
                parts.at[c, 1 - y, :, rows],
                from_y.at[:, rows],
                send_sem.at[sem],
                recv_sem.at[sem],
                me + 2 - 4 * y,
            )
        )
        for zz in range(NZ):
            add_into(parts.at[c, y, zz, rows], from_core.at[y, zz, rows])
    third = []
    for k, rows in enumerate(chunks):
        second[k].wait_recv()
        sent = []
        for step in range(1, NZ):
            to = (z + step) % NZ
            add_into(parts.at[c, y, to, rows], from_y.at[to, rows])
            sem = 5 * k + 1 + step
            sent.append(
                send(
                    parts.at[c, y, to, rows],
                    from_z.at[step - 1, rows],
                    send_sem.at[sem],
                    recv_sem.at[sem],
                    to * 4 + y * 2 + c,
                )
            )
        third.append(sent)
    for k, rows in enumerate(chunks):
        total = parts[c, y, z, rows].astype(jnp.float32) + from_y[z, rows].astype(jnp.float32)
        for step in range(1, NZ):
            third[k][step - 1].wait_recv()
            total = total + from_z[step - 1, rows].astype(jnp.float32)
        finish(k, rows, total)
        copies += third[k]
    return first + second + copies


def all_gather(blocks, send_sem, recv_sem):
    me, z, y, c = place()
    chunks = row_chunks(blocks.shape[3])
    first = []
    for k, rows in enumerate(chunks):
        own = blocks.at[c, y, z, rows]
        first.append(
            [
                send(
                    own,
                    own,
                    send_sem.at[5 * k + step - 1],
                    recv_sem.at[5 * k + step - 1],
                    ((z + step) % NZ) * 4 + y * 2 + c,
                )
                for step in range(1, NZ)
            ]
        )
    second = []
    for k, rows in enumerate(chunks):
        for copy in first[k]:
            copy.wait_recv()
        own = blocks.at[c, y, :, rows]
        second.append(
            send(own, own, send_sem.at[5 * k + 3], recv_sem.at[5 * k + 3], me + 2 - 4 * y)
        )
    third = []
    for k, rows in enumerate(chunks):
        second[k].wait_recv()
        own = blocks.at[c, :, :, rows]
        third.append(
            send(own, own, send_sem.at[5 * k + 4], recv_sem.at[5 * k + 4], me + 1 - 2 * c)
        )
    for copy in third:
        copy.wait_recv()
    return [copy for group in first for copy in group] + second + third


def project_kernel(
    tokens,
    gain,
    w_hbm,
    q_all,
    kv_own,
    w_qkv,
    stats,
    parts,
    from_core,
    from_y,
    from_z,
    stat_send,
    stat_recv,
    rs_send,
    rs_recv,
    ag_send,
    ag_recv,
    load_sem,
):
    load = pltpu.make_async_copy(w_hbm, w_qkv, load_sem)
    load.start()
    me, z, y, c = place()
    greet_all(False)
    token_float = tokens[...].astype(jnp.float32)
    stat_copies = start_stats(token_float, stats, stat_send, stat_recv)
    mean, scale = finish_stats(stat_copies, stats)
    normed = ((token_float - mean) * scale * gain[...]).astype(jnp.bfloat16)
    load.wait()
    for head in range(NSEQ):
        columns = pl.ds(head * 128, 128)
        for part in range(3):
            parts[head % 2, (head // 2) % 2, head // 4, :, part * 128 : part * 128 + 128] = jnp.dot(
                normed, w_qkv[part, :, columns], preferred_element_type=jnp.float32
            ).astype(jnp.bfloat16)

    def finish(k, rows, total):
        joined = total.astype(jnp.bfloat16)
        q_all[c, y, z, rows] = joined[:, :128]
        kv_own[rows] = joined

    copies = reduce_scatter(parts, from_core, from_y, from_z, rs_send, rs_recv, finish)
    copies += all_gather(q_all, ag_send, ag_recv)
    for copy in stat_copies + copies:
        copy.wait_send()


def project(tokens, gain, w_qkv):
    rows = tokens.shape[0]
    width = 384
    vmem = pl.BlockSpec(memory_space=pltpu.VMEM)
    dma = pltpu.SemaphoreType.DMA
    bf16 = jnp.bfloat16
    return pl.pallas_call(
        project_kernel,
        out_shape=(
            jax.ShapeDtypeStruct((2, 2, NZ, rows, 128), bf16),
            jax.ShapeDtypeStruct((rows, width), bf16),
        ),
        in_specs=[vmem, vmem, pl.BlockSpec(memory_space=pl.ANY)],
        out_specs=(vmem, vmem),
        scratch_shapes=[
            pltpu.VMEM(w_qkv.shape, bf16),
            pltpu.VMEM((NSEQ, 16, rows), jnp.float32),
            pltpu.VMEM((2, 2, NZ, rows, width), bf16),
            pltpu.VMEM((2, NZ, rows, width), bf16),
            pltpu.VMEM((NZ, rows, width), bf16),
            pltpu.VMEM((NZ - 1, rows, width), bf16),
            dma((NSEQ - 1,)),
            dma((NSEQ - 1,)),
            dma((5 * CHUNKS,)),
            dma((5 * CHUNKS,)),
            dma((5 * CHUNKS,)),
            dma((5 * CHUNKS,)),
            dma,
        ],
        compiler_params=pltpu.CompilerParams(
            collective_id=0, has_side_effects=True, vmem_limit_bytes=VMEM_LIMIT
        ),
        name="project",
    )(tokens, gain, w_qkv)


PAGES_STEP = 8


def pages_kernel(owners, numbers, lengths, q_all, slopes, keys, values, out, marks, q_rows):
    turn = pl.program_id(0)
    requests = lengths.shape[0]
    nheads = NSEQ
    width = nheads * 128
    page_len = keys.shape[1]
    root = 128 ** (-0.5)

    @pl.when(turn == 0)
    def _():
        for head in range(nheads):
            q_rows[:, head * 128 : head * 128 + 128] = q_all[
                head % 2, (head // 2) % 2, head // 4
            ].astype(jnp.float32)
        marks[...] = jnp.full_like(marks, -1.0)

    own_head = lax.broadcasted_iota(jnp.int32, (nheads, width), 0) == (
        lax.broadcasted_iota(jnp.int32, (nheads, width), 1) // 128
    )
    slope = jnp.sum(
        jnp.where(
            lax.broadcasted_iota(jnp.int32, (nheads, nheads), 0)
            == lax.broadcasted_iota(jnp.int32, (nheads, nheads), 1),
            slopes[...],
            0.0,
        ),
        axis=1,
        keepdims=True,
    )
    slope = jnp.concatenate([slope, slope], axis=0)
    step_row = lax.broadcasted_iota(jnp.int32, (2 * nheads, page_len), 0) // nheads
    offset = lax.broadcasted_iota(jnp.int32, (2 * nheads, page_len), 1)
    lane = lax.broadcasted_iota(jnp.int32, (nheads, 128), 1)
    top_rows = marks[:, 0, :]
    sum_rows = marks[:, 1, :]
    owner_rows = marks[:, 2, :]
    page_outs = []
    for slot in range(PAGES_STEP):
        page = turn * PAGES_STEP + slot
        owner = owners[page]
        safe = jnp.clip(owner, 0, requests - 1)
        left = lengths[safe] - numbers[page] * page_len
        queries = [
            jnp.where(own_head, q_rows[pl.ds(safe + step * requests, 1), :], 0.0)
            for step in range(2)
        ]
        spread = jnp.concatenate(queries, axis=0).astype(jnp.bfloat16)
        scores = lax.dot_general(
            spread, keys[slot], (((1,), (1,)), ((), ())), preferred_element_type=jnp.float32
        )
        distance = (left + step_row - offset).astype(jnp.float32)
        scores = scores * root - distance * slope
        valid = (offset < left) & (owner >= 0)
        masked = jnp.where(valid, scores, floor_score)
        top = jnp.max(masked, axis=1, keepdims=True)
        expon = jnp.where(valid, jnp.exp(masked - top), 0.0)
        total = jnp.sum(expon, axis=1, keepdims=True)
        mixed = jnp.dot(
            expon.astype(jnp.bfloat16), values[slot], preferred_element_type=jnp.float32
        )
        for step in range(2):
            rows = slice(step * nheads, (step + 1) * nheads)
            page_outs.append(
                jnp.sum(jnp.where(own_head, mixed[rows], 0.0), axis=0, keepdims=True)
            )
            here = lane == 2 * page + step
            top_rows = jnp.where(here, top[rows], top_rows)
            sum_rows = jnp.where(here, total[rows], sum_rows)
            owner_rows = jnp.where(here, owner.astype(jnp.float32), owner_rows)
    marks[:, 0, :] = top_rows
    marks[:, 1, :] = sum_rows
    marks[:, 2, :] = owner_rows
    stacked = jnp.concatenate(page_outs, axis=0).astype(jnp.bfloat16)
    first = pl.multiple_of(turn * 2 * PAGES_STEP, 2 * PAGES_STEP)
    for head in range(nheads):
        out[head, pl.ds(first, 2 * PAGES_STEP), :] = stacked[:, head * 128 : head * 128 + 128]


def attend_pages(page_owner, page_number, lengths, q_all, slopes, key_pages, value_pages):
    npages, page_len, width = key_pages.shape
    rows = q_all.shape[3]
    block = pl.BlockSpec((PAGES_STEP, page_len, width), lambda i, *_: (i, 0, 0))
    return pl.pallas_call(
        pages_kernel,
        grid_spec=pltpu.PrefetchScalarGridSpec(
            num_scalar_prefetch=3,
            grid=(npages // PAGES_STEP,),
            in_specs=[
                pl.BlockSpec(q_all.shape, lambda i, *_: (0, 0, 0, 0, 0)),
                pl.BlockSpec(slopes.shape, lambda i, *_: (0, 0)),
                block,
                block,
            ],
            out_specs=(
                pl.BlockSpec((NSEQ, 2 * npages, 128), lambda i, *_: (0, 0, 0)),
                pl.BlockSpec((NSEQ, 8, 128), lambda i, *_: (0, 0, 0)),
            ),
            scratch_shapes=[pltpu.VMEM((rows, width), jnp.float32)],
        ),
        out_shape=(
            jax.ShapeDtypeStruct((NSEQ, 2 * npages, 128), jnp.bfloat16),
            jax.ShapeDtypeStruct((NSEQ, 8, 128), jnp.float32),
        ),
        compiler_params=pltpu.CompilerParams(
            vmem_limit_bytes=VMEM_LIMIT, dimension_semantics=("arbitrary",)
        ),
        name="attend_pages",
    )(page_owner, page_number, lengths, q_all, slopes, key_pages, value_pages)


def combine(qkv, slopes, page_out, marks):
    rows = qkv.shape[0]
    requests = rows // 2
    me = lax.axis_index("seq")
    joined = qkv[...].astype(jnp.float32)
    query, new_key, new_value = joined[:, :128], joined[:, 128:256], joined[:, 256:]
    slope = jnp.sum(
        jnp.where(lax.broadcasted_iota(jnp.int32, slopes.shape, 1) == me, slopes[...], 0.0),
        axis=1,
        keepdims=True,
    )
    root = 128 ** (-0.5)
    same = jnp.sum(query * new_key, axis=1, keepdims=True) * root
    key_before = jnp.concatenate([new_key[:requests], new_key[:requests]], axis=0)
    value_before = jnp.concatenate([new_value[:requests], new_value[:requests]], axis=0)
    later = lax.broadcasted_iota(jnp.int32, (rows, 1), 0) >= requests
    before = jnp.where(
        later, jnp.sum(query * key_before, axis=1, keepdims=True) * root - slope, floor_score
    )
    row_id = lax.broadcasted_iota(jnp.int32, (rows, 128), 0)
    lane_step = lax.broadcasted_iota(jnp.int32, (rows, 128), 1) % 2
    row_step = row_id // requests
    row_owner = (row_id % requests).astype(jnp.float32)

    def member(source):
        return (marks[source, 2:3, :] == row_owner) & (lane_step == row_step)

    best = jnp.full((rows, 128), floor_score, jnp.float32)
    for source in range(NSEQ):
        best = jnp.maximum(best, jnp.where(member(source), marks[source, 0:1, :], floor_score))
    top = jnp.maximum(jnp.max(best, axis=1, keepdims=True), jnp.maximum(same, before))
    e_same = jnp.exp(same - top)
    e_before = jnp.where(later, jnp.exp(before - top), 0.0)
    sums = jnp.zeros((rows, 128), jnp.float32)
    mixed = e_same.astype(jnp.bfloat16).astype(jnp.float32) * new_value + e_before.astype(
        jnp.bfloat16
    ).astype(jnp.float32) * value_before
    live = page_out.shape[1]
    for source in range(NSEQ):
        factor = jnp.where(member(source), jnp.exp(marks[source, 0:1, :] - top), 0.0)
        sums = sums + factor * marks[source, 1:2, :]
        mixed = mixed + jnp.dot(
            factor[:, :live].astype(jnp.bfloat16),
            page_out[source],
            preferred_element_type=jnp.float32,
        )
    total = jnp.sum(sums, axis=1, keepdims=True) + e_same + e_before
    return (mixed / total).astype(jnp.bfloat16)


def finish_kernel(
    tokens,
    qkv,
    slopes,
    gain,
    page_out,
    marks,
    w_out_hbm,
    w_up_hbm,
    w_down_hbm,
    result,
    w_out,
    w_up,
    w_down,
    got_out,
    got_marks,
    attended,
    pair_out,
    stats,
    parts,
    from_core,
    from_y,
    from_z,
    hidden,
    ex_send,
    ex_recv,
    pair_send,
    pair_recv,
    stat_send,
    stat_recv,
    rs_send,
    rs_recv,
    ag_send,
    ag_recv,
    load_sem,
):
    loads = [
        pltpu.make_async_copy(src, dst, load_sem.at[n])
        for n, (src, dst) in enumerate(
            ((w_out_hbm, w_out), (w_up_hbm, w_up), (w_down_hbm, w_down))
        )
    ]
    for load in loads:
        load.start()
    me, z, y, c = place()
    other = 1 - lax.axis_index("head")
    greet_all(True)
    copies = []
    for step in range(1, NSEQ):
        to = (me + step) % NSEQ
        n = 2 * (step - 1)
        copies.append(
            send(page_out.at[to], got_out.at[me], ex_send.at[n], ex_recv.at[n], to)
        )
        copies.append(
            send(marks.at[to], got_marks.at[me], ex_send.at[n + 1], ex_recv.at[n + 1], to)
        )
    got_out[me] = page_out[me]
    got_marks[me] = marks[me]
    for copy in copies:
        copy.wait_recv()
    attended[c, y, z] = combine(qkv, slopes, got_out, got_marks)
    copies += all_gather(attended, ag_send.at[0], ag_recv.at[0])
    contract = (((1,), (1,)), ((), ()))
    loads[0].wait()
    projected = jnp.zeros(pair_out.shape[2:], jnp.float32)
    for head in range(NSEQ):
        projected = projected + lax.dot_general(
            attended[head % 2, (head // 2) % 2, head // 4],
            w_out[:, head * 128 : head * 128 + 128],
            contract,
            preferred_element_type=jnp.float32,
        )
    pair_out[0, 0] = projected
    pair = send(
        pair_out.at[0, 0], pair_out.at[0, 1], pair_send.at[0], pair_recv.at[0], other, "head"
    )
    copies.append(pair)
    pair.wait_recv()
    hidden_in = (
        tokens[...].astype(jnp.float32) + (projected + pair_out[0, 1])
    ).astype(jnp.bfloat16)
    hidden_float = hidden_in.astype(jnp.float32)
    stat_copies = start_stats(hidden_float, stats, stat_send, stat_recv)
    copies += stat_copies
    mean, scale = finish_stats(stat_copies, stats)
    normed = ((hidden_float - mean) * scale * gain[...]).astype(jnp.bfloat16)
    loads[1].wait()
    share = parts.shape[4]
    for block in range(NSEQ):
        parts[block % 2, (block // 2) % 2, block // 4] = jnp.dot(
            normed,
            w_up[:, block * share : (block + 1) * share],
            preferred_element_type=jnp.float32,
        ).astype(jnp.bfloat16)

    def finish(k, rows, total):
        hidden[c, y, z, rows] = (0.5 * total * (1.0 + lax.erf(total * 0.5**0.5))).astype(
            jnp.bfloat16
        )

    copies += reduce_scatter(parts, from_core, from_y, from_z, rs_send, rs_recv, finish)
    copies += all_gather(hidden, ag_send.at[1], ag_recv.at[1])
    loads[2].wait()
    down = jnp.zeros(pair_out.shape[2:], jnp.float32)
    for block in range(NSEQ):
        down = down + lax.dot_general(
            hidden[block % 2, (block // 2) % 2, block // 4],
            w_down[:, block * share : (block + 1) * share],
            contract,
            preferred_element_type=jnp.float32,
        )
    pair_out[1, 0] = down
    pair = send(
        pair_out.at[1, 0], pair_out.at[1, 1], pair_send.at[1], pair_recv.at[1], other, "head"
    )
    copies.append(pair)
    pair.wait_recv()
    result[...] = (hidden_float + (down + pair_out[1, 1])).astype(jnp.bfloat16)
    for copy in copies:
        copy.wait_send()


def finish_layer(tokens, qkv, slopes, gain, page_out, marks, w_out, w_up, w_down):
    rows, local_width = tokens.shape
    share = w_up.shape[1] // NSEQ
    vmem = pl.BlockSpec(memory_space=pltpu.VMEM)
    hbm = pl.BlockSpec(memory_space=pl.ANY)
    dma = pltpu.SemaphoreType.DMA
    bf16 = jnp.bfloat16
    return pl.pallas_call(
        finish_kernel,
        out_shape=jax.ShapeDtypeStruct((rows, local_width), bf16),
        in_specs=[vmem] * 6 + [hbm] * 3,
        out_specs=vmem,
        scratch_shapes=[
            pltpu.VMEM(w_out.shape, bf16),
            pltpu.VMEM(w_up.shape, bf16),
            pltpu.VMEM(w_down.shape, bf16),
            pltpu.VMEM(page_out.shape, bf16),
            pltpu.VMEM(marks.shape, jnp.float32),
            pltpu.VMEM((2, 2, NZ, rows, 128), bf16),
            pltpu.VMEM((2, 2, rows, local_width), jnp.float32),
            pltpu.VMEM((NSEQ, 16, rows), jnp.float32),
            pltpu.VMEM((2, 2, NZ, rows, share), bf16),
            pltpu.VMEM((2, NZ, rows, share), bf16),
            pltpu.VMEM((NZ, rows, share), bf16),
            pltpu.VMEM((NZ - 1, rows, share), bf16),
            pltpu.VMEM((2, 2, NZ, rows, share), bf16),
            dma((2 * NSEQ - 2,)),
            dma((2 * NSEQ - 2,)),
            dma((2,)),
            dma((2,)),
            dma((NSEQ - 1,)),
            dma((NSEQ - 1,)),
            dma((5 * CHUNKS,)),
            dma((5 * CHUNKS,)),
            dma((2, 5 * CHUNKS)),
            dma((2, 5 * CHUNKS)),
            dma((3,)),
        ],
        compiler_params=pltpu.CompilerParams(
            collective_id=1, has_side_effects=True, vmem_limit_bytes=VMEM_LIMIT
        ),
        name="finish_layer",
    )(tokens, qkv, slopes, gain, page_out, marks, w_out, w_up, w_down)


def on_device_kernels(
    tokens,
    lengths,
    page_owner,
    page_number,
    key_pages,
    value_pages,
    alibi_slopes,
    norm1_gain,
    norm2_gain,
    w_qkv,
    w_out,
    w_up,
    w_down,
):
    nsteps, requests, local_width = tokens.shape
    rows = tokens.reshape(nsteps * requests, local_width)
    slopes = alibi_slopes[None, :]
    q_all, qkv = project(rows, norm1_gain[None, :], jnp.transpose(w_qkv, (1, 0, 2)))
    page_out, marks = attend_pages(
        page_owner, page_number, lengths, q_all, slopes, key_pages, value_pages
    )
    result = finish_layer(
        rows, qkv, slopes, norm2_gain[None, :], page_out, marks, w_out, w_up, w_down
    )
    return result.reshape(tokens.shape)


def solution(mesh):
    placed = (
        P(None, None, "seq"),
        P(),
        P("seq"),
        P("seq"),
        P("seq", None, "head"),
        P("seq", None, "head"),
        P("head"),
        P("seq"),
        P("seq"),
        P("seq", None, "head"),
        P("seq", "head"),
        P("seq", "head"),
        P("seq", "head"),
    )
    fits = mesh.shape["seq"] == NSEQ and mesh.shape["head"] == 2
    return jax.shard_map(
        on_device_kernels if fits else on_device, mesh=mesh, in_specs=placed, out_specs=P(None, None, "seq"), check_vma=False
    )
```

```python
import functools

import jax
import jax.numpy as jnp
from jax import lax
from jax.experimental import pallas as pl
from jax.experimental.pallas import tpu as pltpu
from jax.sharding import PartitionSpec as P

D = 4096
BLK = 8


eps_norm = 1e-05
floor_score = -1e30
highest = lax.Precision.HIGHEST


def normalize(token_rows, gain_share, totals, width_all):
    row_sum, row_squares = totals
    mean_value = row_sum / width_all
    variance = row_squares / width_all - mean_value * mean_value
    return (
        (token_rows.astype(jnp.float32) - mean_value[:, None])
        * lax.rsqrt(variance + eps_norm)[:, None]
        * gain_share[None, :]
    ).astype(jnp.bfloat16)


def page_block(
    carry_state, owners, number, key_block, value_block, queries, slopes, lengths, token_step
):
    run_max, run_sum, run_out = carry_state
    nblock, page_len, width_all = key_block.shape
    nheads = slopes.shape[0]
    head_size = width_all // nheads
    requests = queries.shape[0]
    safe_owner = jnp.clip(owners, 0, requests - 1)
    page_query = jnp.take(queries, safe_owner, axis=0)
    key_heads = key_block.reshape(nblock, page_len, nheads, head_size)
    value_heads = value_block.reshape(nblock, page_len, nheads, head_size)
    scores = jnp.einsum(
        "bhe,bthe->bth", page_query, key_heads, preferred_element_type=jnp.float32
    ) * head_size ** (-0.5)
    positions = number[:, None] * page_len + jnp.arange(page_len, dtype=jnp.int32)[None, :]
    own_length = jnp.take(lengths, safe_owner)
    distance = (own_length[:, None] + token_step - positions).astype(jnp.float32)
    scores = scores - distance[:, :, None] * slopes[None, None, :]
    valid_mask = (owners[:, None] >= 0) & (positions < own_length[:, None])
    masked = jnp.where(valid_mask[:, :, None], scores, floor_score)
    page_max = jnp.max(masked, axis=1)
    member = owners[None, :] == jnp.arange(requests, dtype=jnp.int32)[:, None]
    block_max = jnp.max(jnp.where(member[:, :, None], page_max[None, :, :], floor_score), axis=1)
    next_max = jnp.maximum(run_max, block_max)
    owner_max = jnp.take(next_max, safe_owner, axis=0)
    expon = jnp.where(valid_mask[:, :, None], jnp.exp(masked - owner_max[:, None, :]), 0.0)
    page_sum = jnp.sum(expon, axis=1)
    weights = expon.astype(jnp.bfloat16)
    page_out = jnp.einsum("bth,bthe->bhe", weights, value_heads, preferred_element_type=jnp.float32)
    member_float = member.astype(jnp.float32)
    rescale = jnp.exp(run_max - next_max)
    next_sum = run_sum * rescale + jnp.dot(member_float, page_sum, precision=highest)
    added = jnp.dot(member_float, page_out.reshape(nblock, nheads * head_size), precision=highest)
    next_out = run_out * rescale[:, :, None] + added.reshape(requests, nheads, head_size)
    return (next_max, next_sum, next_out)


def attend_new(carry_state, queries, new_keys, new_values, slopes, token_step):
    run_max, run_sum, run_out = carry_state
    head_size = queries.shape[2]
    for earlier in range(token_step + 1):
        scores = jnp.sum(
            queries.astype(jnp.float32) * new_keys[earlier].astype(jnp.float32), axis=2
        ) * head_size ** (-0.5)
        scores = scores - slopes[None, :] * float(token_step - earlier)
        next_max = jnp.maximum(run_max, scores)
        rescale = jnp.exp(run_max - next_max)
        expon = jnp.exp(scores - next_max)
        weights = lax.optimization_barrier(expon.astype(jnp.bfloat16)).astype(jnp.float32)
        run_sum = run_sum * rescale + expon
        run_out = run_out * rescale[:, :, None] + weights[:, :, None] * new_values[earlier].astype(
            jnp.float32
        )
        run_max = next_max
    attended = (run_out / run_sum[:, :, None]).astype(jnp.bfloat16)
    return attended.reshape(attended.shape[0], -1)


def on_device(
    tokens,
    lengths,
    page_owner,
    page_number,
    key_pages,
    value_pages,
    alibi_slopes,
    norm1_gain,
    norm2_gain,
    w_qkv,
    w_out,
    w_up,
    w_down,
):
    nsteps, requests, local_width = tokens.shape
    nheads = alibi_slopes.shape[0]
    head_width = key_pages.shape[2]
    head_size = head_width // nheads
    nblocks = key_pages.shape[0] // BLK
    qkv_width = w_qkv.shape[1] * w_qkv.shape[2]
    new_keys = []
    new_values = []
    outputs = []
    for token_step in range(nsteps):
        token_rows = tokens[token_step]
        token_float = token_rows.astype(jnp.float32)
        totals = lax.psum(
            (jnp.sum(token_float, axis=1), jnp.sum(token_float * token_float, axis=1)), "seq"
        )
        normed = normalize(token_rows, norm1_gain, totals, D)
        partial_qkv = jnp.dot(
            normed, w_qkv.reshape(local_width, qkv_width), preferred_element_type=jnp.float32
        )
        joined = lax.psum(partial_qkv, "seq").astype(jnp.bfloat16)
        queries = joined[:, :head_width].reshape(requests, nheads, head_size)
        new_keys.append(joined[:, head_width : 2 * head_width].reshape(requests, nheads, head_size))
        new_values.append(joined[:, 2 * head_width :].reshape(requests, nheads, head_size))
        carry_state = (
            jnp.full((requests, nheads), floor_score, jnp.float32),
            jnp.zeros((requests, nheads), jnp.float32),
            jnp.zeros((requests, nheads, head_size), jnp.float32),
        )

        def visit(turn_index, state_in):
            first_page = (turn_index * BLK).astype(jnp.int32)
            owners = lax.dynamic_slice_in_dim(page_owner, first_page, BLK, 0)
            number = lax.dynamic_slice_in_dim(page_number, first_page, BLK, 0)
            key_block = lax.dynamic_slice_in_dim(key_pages, first_page, BLK, 0)
            value_block = lax.dynamic_slice_in_dim(value_pages, first_page, BLK, 0)

            def compute(state_given):
                return page_block(
                    state_given,
                    owners,
                    number,
                    key_block,
                    value_block,
                    queries,
                    alibi_slopes,
                    lengths,
                    token_step,
                )

            def keep_state(state_given):
                return state_given

            return lax.cond(jnp.any(owners >= 0), compute, keep_state, state_in)

        carry_state = lax.fori_loop(0, nblocks, visit, carry_state)
        run_max, run_sum, run_out = carry_state
        top_max = lax.pmax(run_max, "seq")
        rescale = jnp.exp(run_max - top_max)
        run_sum, run_out = lax.psum((run_sum * rescale, run_out * rescale[:, :, None]), "seq")
        run_max = top_max
        attended = attend_new(
            (run_max, run_sum, run_out), queries, new_keys, new_values, alibi_slopes, token_step
        )
        projected = lax.psum(
            lax.dot_general(
                attended, w_out, (((1,), (1,)), ((), ())), preferred_element_type=jnp.float32
            ),
            "head",
        )
        hidden_in = (token_float + projected).astype(jnp.bfloat16)
        hidden_float = hidden_in.astype(jnp.float32)
        totals_two = lax.psum(
            (jnp.sum(hidden_float, axis=1), jnp.sum(hidden_float * hidden_float, axis=1)), "seq"
        )
        normed_two = normalize(hidden_in, norm2_gain, totals_two, D)
        up_proj = jnp.dot(normed_two, w_up, preferred_element_type=jnp.float32)
        up_share = lax.psum_scatter(up_proj, "seq", scatter_dimension=1, tiled=True)
        hidden_share = jax.nn.gelu(up_share, approximate=False).astype(jnp.bfloat16)
        down_part = lax.dot_general(
            lax.all_gather(hidden_share, "seq", axis=1, tiled=True),
            w_down,
            (((1,), (1,)), ((), ())),
            preferred_element_type=jnp.float32,
        )
        down_proj = lax.psum(down_part, "head")
        outputs.append((hidden_float + down_proj).astype(jnp.bfloat16))
    return jnp.stack(outputs)

MESH = pl.DeviceIdType.MESH
NSEQ = 16
NZ = 4
COPIES = 3 * NZ - 1
VMEM_LIMIT = 60 * 1024 * 1024


def place():
    index = lax.axis_index("seq")
    return index, index // 4, (index // 2) % 2, index % 2


def send(src, dst, send_sem, recv_sem, peer, axis="seq"):
    copy = pltpu.make_async_remote_copy(
        src_ref=src,
        dst_ref=dst,
        send_sem=send_sem,
        recv_sem=recv_sem,
        device_id={axis: peer},
        device_id_type=MESH,
    )
    copy.start()
    return copy


def greet_all(with_head):
    me = lax.axis_index("seq")
    barrier = pltpu.get_barrier_semaphore()
    for step in range(1, NSEQ):
        pl.semaphore_signal(
            barrier, inc=1, device_id={"seq": (me + step) % NSEQ}, device_id_type=MESH
        )
    if with_head:
        other = 1 - lax.axis_index("head")
        pl.semaphore_signal(barrier, inc=1, device_id={"head": other}, device_id_type=MESH)
    pl.semaphore_wait(barrier, NSEQ - 1 + int(with_head))


def row_to_column(row):
    width = row.shape[1]
    same = lax.broadcasted_iota(jnp.int32, (width, width), 0) == lax.broadcasted_iota(
        jnp.int32, (width, width), 1
    )
    return jnp.sum(jnp.where(same, row, 0.0), axis=1, keepdims=True)


def start_stats(values, stats, send_sem, recv_sem):
    me = lax.axis_index("seq")
    ones = jnp.ones((8, values.shape[1]), jnp.float32)
    contract = (((1,), (1,)), ((), ()))
    stats[me, 0:8, :] = lax.dot_general(
        ones, values, contract, precision=highest, preferred_element_type=jnp.float32
    )
    stats[me, 8:16, :] = lax.dot_general(
        ones, values * values, contract, precision=highest, preferred_element_type=jnp.float32
    )
    return [
        send(
            stats.at[me],
            stats.at[me],
            send_sem.at[step - 1],
            recv_sem.at[step - 1],
            (me + step) % NSEQ,
        )
        for step in range(1, NSEQ)
    ]


def finish_stats(copies, stats):
    for copy in copies:
        copy.wait_recv()
    total = stats[0]
    for source in range(1, NSEQ):
        total = total + stats[source]
    mean = total[0:1, :] / D
    variance = total[8:9, :] / D - mean * mean
    return row_to_column(mean), row_to_column(lax.rsqrt(variance + eps_norm))


def add_into(target, extra):
    target[...] = (target[...].astype(jnp.float32) + extra[...].astype(jnp.float32)).astype(
        jnp.bfloat16
    )


def reduce_scatter(parts, from_core, from_y, from_z, send_sem, recv_sem, produce):
    me, z, y, c = place()
    turns = [(z + 1 + turn) % NZ for turn in range(NZ)]
    first, second, third = [], [], []
    for turn, to in enumerate(turns):
        produce(1 - c, to)
        first.append(
            send(
                parts.at[1 - c, to],
                from_core.at[to],
                send_sem.at[turn],
                recv_sem.at[turn],
                me + 1 - 2 * c,
            )
        )
    for to in turns:
        produce(c, to)

    def pass_z(turn):
        to = turns[turn]
        second[turn].wait_recv()
        add_into(parts.at[c, to, y], from_y.at[to])
        third.append(
            send(
                parts.at[c, to, y],
                from_z.at[turn],
                send_sem.at[2 * NZ + turn],
                recv_sem.at[2 * NZ + turn],
                to * 4 + y * 2 + c,
            )
        )

    for turn, to in enumerate(turns):
        first[turn].wait_recv()
        add_into(parts.at[c, to, 1 - y], from_core.at[to, 1 - y])
        second.append(
            send(
                parts.at[c, to, 1 - y],
                from_y.at[to],
                send_sem.at[NZ + turn],
                recv_sem.at[NZ + turn],
                me + 2 - 4 * y,
            )
        )
        if turn < NZ - 1:
            add_into(parts.at[c, to, y], from_core.at[to, y])
        if turn > 0:
            pass_z(turn - 1)
    second[NZ - 1].wait_recv()
    total = (
        parts[c, z, y].astype(jnp.float32)
        + from_core[z, y].astype(jnp.float32)
        + from_y[z].astype(jnp.float32)
    )
    for turn in range(NZ - 1):
        third[turn].wait_recv()
        total = total + from_z[turn].astype(jnp.float32)
    return total, first + second + third


def all_gather(blocks, send_sem, recv_sem, consume):
    me, z, y, c = place()
    own = blocks.at[c, z, y]
    turns = [(z + NZ - turn) % NZ for turn in range(NZ)]
    along_z = [
        send(
            own,
            own,
            send_sem.at[turn - 1],
            recv_sem.at[turn - 1],
            ((z + turn) % NZ) * 4 + y * 2 + c,
        )
        for turn in range(1, NZ)
    ]
    along_y, across = [], []

    def pass_y(turn):
        block = blocks.at[c, turns[turn], y]
        sem = NZ - 1 + turn
        along_y.append(send(block, block, send_sem.at[sem], recv_sem.at[sem], me + 2 - 4 * y))

    def pass_core(turn):
        along_y[turn].wait_recv()
        block = blocks.at[c, turns[turn]]
        sem = 2 * NZ - 1 + turn
        across.append(send(block, block, send_sem.at[sem], recv_sem.at[sem], me + 1 - 2 * c))
        consume(c, turns[turn])

    pass_y(0)
    for turn in range(1, NZ):
        along_z[turn - 1].wait_recv()
        pass_y(turn)
        pass_core(turn - 1)
    pass_core(NZ - 1)
    for turn in range(NZ):
        across[turn].wait_recv()
        consume(1 - c, turns[turn])
    return along_z + along_y + across


def columns_of(core, to, y, width):
    return pl.ds(pl.multiple_of((to * 4 + y * 2 + core) * width, width), width)


def project_kernel(
    tokens,
    gain,
    w_hbm,
    q_all,
    kv_own,
    w_qkv,
    stats,
    parts,
    from_core,
    from_y,
    from_z,
    stat_send,
    stat_recv,
    rs_send,
    rs_recv,
    ag_send,
    ag_recv,
    load_sem,
):
    load = pltpu.make_async_copy(w_hbm, w_qkv, load_sem)
    load.start()
    me, z, y, c = place()
    greet_all(False)
    token_float = tokens[...].astype(jnp.float32)
    stat_copies = start_stats(token_float, stats, stat_send, stat_recv)
    mean, scale = finish_stats(stat_copies, stats)
    normed = ((token_float - mean) * scale * gain[...]).astype(jnp.bfloat16)
    load.wait()

    def produce(core, to):
        for side in range(2):
            columns = columns_of(core, to, side, 128)
            weight = jnp.concatenate([w_qkv[part, :, columns] for part in range(3)], axis=1)
            parts[core, to, side] = jnp.dot(
                normed, weight, preferred_element_type=jnp.float32
            ).astype(jnp.bfloat16)

    def consume(core, source):
        del core, source

    total, copies = reduce_scatter(
        parts, from_core, from_y, from_z, rs_send, rs_recv, produce
    )
    joined = total.astype(jnp.bfloat16)
    q_all[c, z, y] = joined[:, :128]
    copies += all_gather(q_all, ag_send, ag_recv, consume)
    kv_own[...] = joined
    for copy in stat_copies + copies:
        copy.wait_send()


def project(tokens, gain, w_qkv):
    rows = tokens.shape[0]
    width = 384
    vmem = pl.BlockSpec(memory_space=pltpu.VMEM)
    dma = pltpu.SemaphoreType.DMA
    bf16 = jnp.bfloat16
    return pl.pallas_call(
        project_kernel,
        out_shape=(
            jax.ShapeDtypeStruct((2, NZ, 2, rows, 128), bf16),
            jax.ShapeDtypeStruct((rows, width), bf16),
        ),
        in_specs=[vmem, vmem, pl.BlockSpec(memory_space=pl.ANY)],
        out_specs=(vmem, vmem),
        scratch_shapes=[
            pltpu.VMEM(w_qkv.shape, bf16),
            pltpu.VMEM((NSEQ, 16, rows), jnp.float32),
            pltpu.VMEM((2, NZ, 2, rows, width), bf16),
            pltpu.VMEM((NZ, 2, rows, width), bf16),
            pltpu.VMEM((NZ, rows, width), bf16),
            pltpu.VMEM((NZ - 1, rows, width), bf16),
            dma((NSEQ - 1,)),
            dma((NSEQ - 1,)),
            dma((COPIES,)),
            dma((COPIES,)),
            dma((COPIES,)),
            dma((COPIES,)),
            dma,
        ],
        compiler_params=pltpu.CompilerParams(
            collective_id=0, has_side_effects=True, vmem_limit_bytes=VMEM_LIMIT
        ),
        name="project",
    )(tokens, gain, w_qkv)


PAGES_STEP = 8


def pages_kernel(
    owners, numbers, lengths, q_all, slopes, keys, values, out, marks, q_rows, tops, totals, owned
):
    turn = pl.program_id(0)
    requests = lengths.shape[0]
    nheads = NSEQ
    page_len = keys.shape[1]
    root = 128 ** (-0.5)
    group = 4
    ngroups = nheads // group
    width = group * 128
    count = 2 * nheads

    @pl.when(turn == 0)
    def _():
        for head in range(nheads):
            q_rows[:, head * 128 : head * 128 + 128] = q_all[
                head % 2, head // 4, (head // 2) % 2
            ].astype(jnp.float32)
        tops[...] = jnp.zeros_like(tops)
        totals[...] = jnp.zeros_like(totals)
        owned[...] = jnp.full_like(owned, -1.0)

    spot = lax.broadcasted_iota(jnp.int32, (2 * group, width), 0)
    own_head = spot % group == lax.broadcasted_iota(jnp.int32, (2 * group, width), 1) // 128
    first_step = spot < group
    row = lax.broadcasted_iota(jnp.int32, (count, nheads), 0)
    row_head = row // (2 * group) * group + row % group
    slope = jnp.sum(
        jnp.where(
            row_head == lax.broadcasted_iota(jnp.int32, (count, nheads), 1), slopes[...], 0.0
        ),
        axis=1,
        keepdims=True,
    )
    step_row = lax.broadcasted_iota(jnp.int32, (count, page_len), 0) // group % 2
    offset = lax.broadcasted_iota(jnp.int32, (count, page_len), 1)
    lane = lax.broadcasted_iota(jnp.int32, (count, 128), 1)
    lane_step = lax.broadcasted_iota(jnp.int32, (count, 128), 0) // group % 2
    lane_one = lax.broadcasted_iota(jnp.int32, (1, 128), 1)
    top_rows = tops[...]
    sum_rows = totals[...]
    owner_row = owned[0:1, :]
    page_outs = []
    for slot in range(PAGES_STEP):
        page = turn * PAGES_STEP + slot
        owner = owners[page]
        safe = jnp.clip(owner, 0, requests - 1)
        left = lengths[safe] - numbers[page] * page_len
        q_first = q_rows[pl.ds(safe, 1), :]
        q_second = q_rows[pl.ds(safe + requests, 1), :]
        scores = []
        for g in range(ngroups):
            columns = slice(g * width, (g + 1) * width)
            spread = jnp.where(
                own_head, jnp.where(first_step, q_first[:, columns], q_second[:, columns]), 0.0
            ).astype(jnp.bfloat16)
            scores.append(
                lax.dot_general(
                    spread,
                    keys[slot, :, columns],
                    (((1,), (1,)), ((), ())),
                    preferred_element_type=jnp.float32,
                )
            )
        distance = (left + step_row - offset).astype(jnp.float32)
        score = jnp.concatenate(scores, axis=0) * root - distance * slope
        valid = (offset < left) & (owner >= 0)
        masked = jnp.where(valid, score, floor_score)
        top = jnp.max(masked, axis=1, keepdims=True)
        expon = jnp.where(valid, jnp.exp(masked - top), 0.0)
        total = jnp.sum(expon, axis=1, keepdims=True)
        mixed = []
        for g in range(ngroups):
            product = jnp.dot(
                expon[g * 2 * group : (g + 1) * 2 * group].astype(jnp.bfloat16),
                values[slot, :, g * width : (g + 1) * width],
                preferred_element_type=jnp.float32,
            )
            mixed.append(jnp.where(own_head, product, 0.0))
        mixed = jnp.concatenate(mixed, axis=1)
        page_outs.append(jnp.sum(mixed[:group], axis=0, keepdims=True))
        page_outs.append(jnp.sum(mixed[group:], axis=0, keepdims=True))
        here = lane == 2 * page + lane_step
        top_rows = jnp.where(here, top, top_rows)
        sum_rows = jnp.where(here, total, sum_rows)
        owner_row = jnp.where(lane_one // 2 == page, owner.astype(jnp.float32), owner_row)
    tops[...] = top_rows
    totals[...] = sum_rows
    owned[0:1, :] = owner_row
    stacked = jnp.concatenate(page_outs, axis=0).astype(jnp.bfloat16)
    first = pl.multiple_of(turn * 2 * PAGES_STEP, 2 * PAGES_STEP)
    for head in range(nheads):
        out[head, pl.ds(first, 2 * PAGES_STEP), :] = stacked[:, head * 128 : head * 128 + 128]

    @pl.when(turn == pl.num_programs(0) - 1)
    def _():
        even = lane_one % 2 == 0
        for head in range(nheads):
            at = head // group * 2 * group + head % group
            for n, rows in enumerate((top_rows, sum_rows)):
                marks[head, n : n + 1, :] = jnp.where(
                    even, rows[at : at + 1], rows[at + group : at + group + 1]
                )
            marks[head, 2:3, :] = owner_row
            marks[head, 3:8, :] = jnp.zeros((5, 128), jnp.float32)


def attend_pages(page_owner, page_number, lengths, q_all, slopes, key_pages, value_pages):
    npages, page_len, width = key_pages.shape
    rows = q_all.shape[3]
    block = pl.BlockSpec((PAGES_STEP, page_len, width), lambda i, *_: (i, 0, 0))
    return pl.pallas_call(
        pages_kernel,
        grid_spec=pltpu.PrefetchScalarGridSpec(
            num_scalar_prefetch=3,
            grid=(npages // PAGES_STEP,),
            in_specs=[
                pl.BlockSpec(q_all.shape, lambda i, *_: (0, 0, 0, 0, 0)),
                pl.BlockSpec(slopes.shape, lambda i, *_: (0, 0)),
                block,
                block,
            ],
            out_specs=(
                pl.BlockSpec((NSEQ, 2 * npages, 128), lambda i, *_: (0, 0, 0)),
                pl.BlockSpec((NSEQ, 8, 128), lambda i, *_: (0, 0, 0)),
            ),
            scratch_shapes=[
                pltpu.VMEM((rows, width), jnp.float32),
                pltpu.VMEM((2 * NSEQ, 128), jnp.float32),
                pltpu.VMEM((2 * NSEQ, 128), jnp.float32),
                pltpu.VMEM((8, 128), jnp.float32),
            ],
        ),
        out_shape=(
            jax.ShapeDtypeStruct((NSEQ, 2 * npages, 128), jnp.bfloat16),
            jax.ShapeDtypeStruct((NSEQ, 8, 128), jnp.float32),
        ),
        compiler_params=pltpu.CompilerParams(
            vmem_limit_bytes=VMEM_LIMIT, dimension_semantics=("arbitrary",)
        ),
        name="attend_pages",
    )(page_owner, page_number, lengths, q_all, slopes, key_pages, value_pages)


def combine(qkv, slopes, page_out, marks):
    rows = qkv.shape[0]
    requests = rows // 2
    me = lax.axis_index("seq")
    joined = qkv[...].astype(jnp.float32)
    query, new_key, new_value = joined[:, :128], joined[:, 128:256], joined[:, 256:]
    slope = jnp.sum(
        jnp.where(lax.broadcasted_iota(jnp.int32, slopes.shape, 1) == me, slopes[...], 0.0),
        axis=1,
        keepdims=True,
    )
    root = 128 ** (-0.5)
    same = jnp.sum(query * new_key, axis=1, keepdims=True) * root
    key_before = jnp.concatenate([new_key[:requests], new_key[:requests]], axis=0)
    value_before = jnp.concatenate([new_value[:requests], new_value[:requests]], axis=0)
    later = lax.broadcasted_iota(jnp.int32, (rows, 1), 0) >= requests
    before = jnp.where(
        later, jnp.sum(query * key_before, axis=1, keepdims=True) * root - slope, floor_score
    )
    row_id = lax.broadcasted_iota(jnp.int32, (rows, 128), 0)
    lane_step = lax.broadcasted_iota(jnp.int32, (rows, 128), 1) % 2
    row_step = row_id // requests
    row_owner = (row_id % requests).astype(jnp.float32)

    def member(source):
        return (marks[source, 2:3, :] == row_owner) & (lane_step == row_step)

    best = jnp.full((rows, 128), floor_score, jnp.float32)
    for source in range(NSEQ):
        best = jnp.maximum(best, jnp.where(member(source), marks[source, 0:1, :], floor_score))
    top = jnp.maximum(jnp.max(best, axis=1, keepdims=True), jnp.maximum(same, before))
    e_same = jnp.exp(same - top)
    e_before = jnp.where(later, jnp.exp(before - top), 0.0)
    sums = jnp.zeros((rows, 128), jnp.float32)
    mixed = e_same.astype(jnp.bfloat16).astype(jnp.float32) * new_value + e_before.astype(
        jnp.bfloat16
    ).astype(jnp.float32) * value_before
    live = page_out.shape[1]
    for source in range(NSEQ):
        factor = jnp.where(member(source), jnp.exp(marks[source, 0:1, :] - top), 0.0)
        sums = sums + factor * marks[source, 1:2, :]
        mixed = mixed + jnp.dot(
            factor[:, :live].astype(jnp.bfloat16),
            page_out[source],
            preferred_element_type=jnp.float32,
        )
    total = jnp.sum(sums, axis=1, keepdims=True) + e_same + e_before
    return (mixed / total).astype(jnp.bfloat16)


def finish_kernel(
    tokens,
    qkv,
    slopes,
    gain,
    page_out,
    marks,
    w_out_hbm,
    w_up_hbm,
    w_down_hbm,
    result,
    w_out,
    w_up,
    w_down,
    got_out,
    got_marks,
    attended,
    pair_out,
    stats,
    parts,
    from_core,
    from_y,
    from_z,
    hidden,
    ex_send,
    ex_recv,
    pair_send,
    pair_recv,
    stat_send,
    stat_recv,
    rs_send,
    rs_recv,
    ag_send,
    ag_recv,
    load_sem,
):
    loads = [
        pltpu.make_async_copy(src, dst, load_sem.at[n])
        for n, (src, dst) in enumerate(
            ((w_out_hbm, w_out), (w_up_hbm, w_up), (w_down_hbm, w_down))
        )
    ]
    for load in loads:
        load.start()
    me, z, y, c = place()
    other = 1 - lax.axis_index("head")
    greet_all(True)
    copies = []
    for step in range(1, NSEQ):
        to = (me + step) % NSEQ
        n = 2 * (step - 1)
        copies.append(
            send(page_out.at[to], got_out.at[me], ex_send.at[n], ex_recv.at[n], to)
        )
        copies.append(
            send(marks.at[to], got_marks.at[me], ex_send.at[n + 1], ex_recv.at[n + 1], to)
        )
    got_out[me] = page_out[me]
    got_marks[me] = marks[me]
    for copy in copies:
        copy.wait_recv()
    attended[c, z, y] = combine(qkv, slopes, got_out, got_marks)
    contract = (((1,), (1,)), ((), ()))
    sums = [jnp.zeros(result.shape, jnp.float32), jnp.zeros(result.shape, jnp.float32)]
    loads[0].wait()

    def consume_attended(core, source):
        for side in range(2):
            sums[0] = sums[0] + lax.dot_general(
                attended[core, source, side],
                w_out[:, columns_of(core, source, side, 128)],
                contract,
                preferred_element_type=jnp.float32,
            )

    copies += all_gather(attended, ag_send.at[0], ag_recv.at[0], consume_attended)
    projected = sums[0].astype(jnp.bfloat16)
    pair_out[0, 0] = projected
    pair = send(
        pair_out.at[0, 0], pair_out.at[0, 1], pair_send.at[0], pair_recv.at[0], other, "head"
    )
    copies.append(pair)
    pair.wait_recv()
    hidden_in = (
        tokens[...].astype(jnp.float32) + (projected.astype(jnp.float32) + pair_out[0, 1].astype(jnp.float32))
    ).astype(jnp.bfloat16)
    hidden_float = hidden_in.astype(jnp.float32)
    stat_copies = start_stats(hidden_float, stats, stat_send, stat_recv)
    copies += stat_copies
    mean, scale = finish_stats(stat_copies, stats)
    normed = ((hidden_float - mean) * scale * gain[...]).astype(jnp.bfloat16)
    loads[1].wait()
    share = parts.shape[4]

    def produce(core, to):
        for side in range(2):
            parts[core, to, side] = jnp.dot(
                normed,
                w_up[:, columns_of(core, to, side, share)],
                preferred_element_type=jnp.float32,
            ).astype(jnp.bfloat16)

    def consume_hidden(core, source):
        for side in range(2):
            sums[1] = sums[1] + lax.dot_general(
                hidden[core, source, side],
                w_down[:, columns_of(core, source, side, share)],
                contract,
                preferred_element_type=jnp.float32,
            )

    total, sent = reduce_scatter(parts, from_core, from_y, from_z, rs_send, rs_recv, produce)
    copies += sent
    hidden[c, z, y] = (0.5 * total * (1.0 + lax.erf(total * 0.5**0.5))).astype(jnp.bfloat16)
    loads[2].wait()
    copies += all_gather(hidden, ag_send.at[1], ag_recv.at[1], consume_hidden)
    down = sums[1].astype(jnp.bfloat16)
    pair_out[1, 0] = down
    pair = send(
        pair_out.at[1, 0], pair_out.at[1, 1], pair_send.at[1], pair_recv.at[1], other, "head"
    )
    copies.append(pair)
    pair.wait_recv()
    result[...] = (hidden_float + (down.astype(jnp.float32) + pair_out[1, 1].astype(jnp.float32))).astype(jnp.bfloat16)
    for copy in copies:
        copy.wait_send()


def finish_layer(tokens, qkv, slopes, gain, page_out, marks, w_out, w_up, w_down):
    rows, local_width = tokens.shape
    share = w_up.shape[1] // NSEQ
    vmem = pl.BlockSpec(memory_space=pltpu.VMEM)
    hbm = pl.BlockSpec(memory_space=pl.ANY)
    dma = pltpu.SemaphoreType.DMA
    bf16 = jnp.bfloat16
    return pl.pallas_call(
        finish_kernel,
        out_shape=jax.ShapeDtypeStruct((rows, local_width), bf16),
        in_specs=[vmem] * 6 + [hbm] * 3,
        out_specs=vmem,
        scratch_shapes=[
            pltpu.VMEM(w_out.shape, bf16),
            pltpu.VMEM(w_up.shape, bf16),
            pltpu.VMEM(w_down.shape, bf16),
            pltpu.VMEM(page_out.shape, bf16),
            pltpu.VMEM(marks.shape, jnp.float32),
            pltpu.VMEM((2, NZ, 2, rows, 128), bf16),
            pltpu.VMEM((2, 2, rows, local_width), bf16),
            pltpu.VMEM((NSEQ, 16, rows), jnp.float32),
            pltpu.VMEM((2, NZ, 2, rows, share), bf16),
            pltpu.VMEM((NZ, 2, rows, share), bf16),
            pltpu.VMEM((NZ, rows, share), bf16),
            pltpu.VMEM((NZ - 1, rows, share), bf16),
            pltpu.VMEM((2, NZ, 2, rows, share), bf16),
            dma((2 * NSEQ - 2,)),
            dma((2 * NSEQ - 2,)),
            dma((2,)),
            dma((2,)),
            dma((NSEQ - 1,)),
            dma((NSEQ - 1,)),
            dma((COPIES,)),
            dma((COPIES,)),
            dma((2, COPIES)),
            dma((2, COPIES)),
            dma((3,)),
        ],
        compiler_params=pltpu.CompilerParams(
            collective_id=1, has_side_effects=True, vmem_limit_bytes=VMEM_LIMIT
        ),
        name="finish_layer",
    )(tokens, qkv, slopes, gain, page_out, marks, w_out, w_up, w_down)


def on_device_kernels(
    tokens,
    lengths,
    page_owner,
    page_number,
    key_pages,
    value_pages,
    alibi_slopes,
    norm1_gain,
    norm2_gain,
    w_qkv,
    w_out,
    w_up,
    w_down,
):
    nsteps, requests, local_width = tokens.shape
    rows = tokens.reshape(nsteps * requests, local_width)
    slopes = alibi_slopes[None, :]
    q_all, qkv = project(rows, norm1_gain[None, :], jnp.transpose(w_qkv, (1, 0, 2)))
    page_out, marks = attend_pages(
        page_owner, page_number, lengths, q_all, slopes, key_pages, value_pages
    )
    result = finish_layer(
        rows, qkv, slopes, norm2_gain[None, :], page_out, marks, w_out, w_up, w_down
    )
    return result.reshape(tokens.shape)


def solution(mesh):
    placed = (
        P(None, None, "seq"),
        P(),
        P("seq"),
        P("seq"),
        P("seq", None, "head"),
        P("seq", None, "head"),
        P("head"),
        P("seq"),
        P("seq"),
        P("seq", None, "head"),
        P("seq", "head"),
        P("seq", "head"),
        P("seq", "head"),
    )
    fits = mesh.shape["seq"] == NSEQ and mesh.shape["head"] == 2
    return jax.shard_map(
        on_device_kernels if fits else on_device, mesh=mesh, in_specs=placed, out_specs=P(None, None, "seq"), check_vma=False
    )
```

```python
import functools

import jax
import jax.numpy as jnp
from jax import lax
from jax.experimental import pallas as pl
from jax.experimental.pallas import tpu as pltpu
from jax.sharding import PartitionSpec as P

D = 4096
BLK = 8


eps_norm = 1e-05
floor_score = -1e30
highest = lax.Precision.HIGHEST


def normalize(token_rows, gain_share, totals, width_all):
    row_sum, row_squares = totals
    mean_value = row_sum / width_all
    variance = row_squares / width_all - mean_value * mean_value
    return (
        (token_rows.astype(jnp.float32) - mean_value[:, None])
        * lax.rsqrt(variance + eps_norm)[:, None]
        * gain_share[None, :]
    ).astype(jnp.bfloat16)


def page_block(
    carry_state, owners, number, key_block, value_block, queries, slopes, lengths, token_step
):
    run_max, run_sum, run_out = carry_state
    nblock, page_len, width_all = key_block.shape
    nheads = slopes.shape[0]
    head_size = width_all // nheads
    requests = queries.shape[0]
    safe_owner = jnp.clip(owners, 0, requests - 1)
    page_query = jnp.take(queries, safe_owner, axis=0)
    key_heads = key_block.reshape(nblock, page_len, nheads, head_size)
    value_heads = value_block.reshape(nblock, page_len, nheads, head_size)
    scores = jnp.einsum(
        "bhe,bthe->bth", page_query, key_heads, preferred_element_type=jnp.float32
    ) * head_size ** (-0.5)
    positions = number[:, None] * page_len + jnp.arange(page_len, dtype=jnp.int32)[None, :]
    own_length = jnp.take(lengths, safe_owner)
    distance = (own_length[:, None] + token_step - positions).astype(jnp.float32)
    scores = scores - distance[:, :, None] * slopes[None, None, :]
    valid_mask = (owners[:, None] >= 0) & (positions < own_length[:, None])
    masked = jnp.where(valid_mask[:, :, None], scores, floor_score)
    page_max = jnp.max(masked, axis=1)
    member = owners[None, :] == jnp.arange(requests, dtype=jnp.int32)[:, None]
    block_max = jnp.max(jnp.where(member[:, :, None], page_max[None, :, :], floor_score), axis=1)
    next_max = jnp.maximum(run_max, block_max)
    owner_max = jnp.take(next_max, safe_owner, axis=0)
    expon = jnp.where(valid_mask[:, :, None], jnp.exp(masked - owner_max[:, None, :]), 0.0)
    page_sum = jnp.sum(expon, axis=1)
    weights = expon.astype(jnp.bfloat16)
    page_out = jnp.einsum("bth,bthe->bhe", weights, value_heads, preferred_element_type=jnp.float32)
    member_float = member.astype(jnp.float32)
    rescale = jnp.exp(run_max - next_max)
    next_sum = run_sum * rescale + jnp.dot(member_float, page_sum, precision=highest)
    added = jnp.dot(member_float, page_out.reshape(nblock, nheads * head_size), precision=highest)
    next_out = run_out * rescale[:, :, None] + added.reshape(requests, nheads, head_size)
    return (next_max, next_sum, next_out)


def attend_new(carry_state, queries, new_keys, new_values, slopes, token_step):
    run_max, run_sum, run_out = carry_state
    head_size = queries.shape[2]
    for earlier in range(token_step + 1):
        scores = jnp.sum(
            queries.astype(jnp.float32) * new_keys[earlier].astype(jnp.float32), axis=2
        ) * head_size ** (-0.5)
        scores = scores - slopes[None, :] * float(token_step - earlier)
        next_max = jnp.maximum(run_max, scores)
        rescale = jnp.exp(run_max - next_max)
        expon = jnp.exp(scores - next_max)
        weights = lax.optimization_barrier(expon.astype(jnp.bfloat16)).astype(jnp.float32)
        run_sum = run_sum * rescale + expon
        run_out = run_out * rescale[:, :, None] + weights[:, :, None] * new_values[earlier].astype(
            jnp.float32
        )
        run_max = next_max
    attended = (run_out / run_sum[:, :, None]).astype(jnp.bfloat16)
    return attended.reshape(attended.shape[0], -1)


def on_device(
    tokens,
    lengths,
    page_owner,
    page_number,
    key_pages,
    value_pages,
    alibi_slopes,
    norm1_gain,
    norm2_gain,
    w_qkv,
    w_out,
    w_up,
    w_down,
):
    nsteps, requests, local_width = tokens.shape
    nheads = alibi_slopes.shape[0]
    head_width = key_pages.shape[2]
    head_size = head_width // nheads
    nblocks = key_pages.shape[0] // BLK
    qkv_width = w_qkv.shape[1] * w_qkv.shape[2]
    new_keys = []
    new_values = []
    outputs = []
    for token_step in range(nsteps):
        token_rows = tokens[token_step]
        token_float = token_rows.astype(jnp.float32)
        totals = lax.psum(
            (jnp.sum(token_float, axis=1), jnp.sum(token_float * token_float, axis=1)), "seq"
        )
        normed = normalize(token_rows, norm1_gain, totals, D)
        partial_qkv = jnp.dot(
            normed, w_qkv.reshape(local_width, qkv_width), preferred_element_type=jnp.float32
        )
        joined = lax.psum(partial_qkv, "seq").astype(jnp.bfloat16)
        queries = joined[:, :head_width].reshape(requests, nheads, head_size)
        new_keys.append(joined[:, head_width : 2 * head_width].reshape(requests, nheads, head_size))
        new_values.append(joined[:, 2 * head_width :].reshape(requests, nheads, head_size))
        carry_state = (
            jnp.full((requests, nheads), floor_score, jnp.float32),
            jnp.zeros((requests, nheads), jnp.float32),
            jnp.zeros((requests, nheads, head_size), jnp.float32),
        )

        def visit(turn_index, state_in):
            first_page = (turn_index * BLK).astype(jnp.int32)
            owners = lax.dynamic_slice_in_dim(page_owner, first_page, BLK, 0)
            number = lax.dynamic_slice_in_dim(page_number, first_page, BLK, 0)
            key_block = lax.dynamic_slice_in_dim(key_pages, first_page, BLK, 0)
            value_block = lax.dynamic_slice_in_dim(value_pages, first_page, BLK, 0)

            def compute(state_given):
                return page_block(
                    state_given,
                    owners,
                    number,
                    key_block,
                    value_block,
                    queries,
                    alibi_slopes,
                    lengths,
                    token_step,
                )

            def keep_state(state_given):
                return state_given

            return lax.cond(jnp.any(owners >= 0), compute, keep_state, state_in)

        carry_state = lax.fori_loop(0, nblocks, visit, carry_state)
        run_max, run_sum, run_out = carry_state
        top_max = lax.pmax(run_max, "seq")
        rescale = jnp.exp(run_max - top_max)
        run_sum, run_out = lax.psum((run_sum * rescale, run_out * rescale[:, :, None]), "seq")
        run_max = top_max
        attended = attend_new(
            (run_max, run_sum, run_out), queries, new_keys, new_values, alibi_slopes, token_step
        )
        projected = lax.psum(
            lax.dot_general(
                attended, w_out, (((1,), (1,)), ((), ())), preferred_element_type=jnp.float32
            ),
            "head",
        )
        hidden_in = (token_float + projected).astype(jnp.bfloat16)
        hidden_float = hidden_in.astype(jnp.float32)
        totals_two = lax.psum(
            (jnp.sum(hidden_float, axis=1), jnp.sum(hidden_float * hidden_float, axis=1)), "seq"
        )
        normed_two = normalize(hidden_in, norm2_gain, totals_two, D)
        up_proj = jnp.dot(normed_two, w_up, preferred_element_type=jnp.float32)
        up_share = lax.psum_scatter(up_proj, "seq", scatter_dimension=1, tiled=True)
        hidden_share = jax.nn.gelu(up_share, approximate=False).astype(jnp.bfloat16)
        down_part = lax.dot_general(
            lax.all_gather(hidden_share, "seq", axis=1, tiled=True),
            w_down,
            (((1,), (1,)), ((), ())),
            preferred_element_type=jnp.float32,
        )
        down_proj = lax.psum(down_part, "head")
        outputs.append((hidden_float + down_proj).astype(jnp.bfloat16))
    return jnp.stack(outputs)

MESH = pl.DeviceIdType.MESH
NSEQ = 16
NZ = 4
COPIES = 3 * NZ - 1
VMEM_LIMIT = 60 * 1024 * 1024


def place():
    index = lax.axis_index("seq")
    return index, index // 4, (index // 2) % 2, index % 2


def send(src, dst, send_sem, recv_sem, peer, axis="seq"):
    copy = pltpu.make_async_remote_copy(
        src_ref=src,
        dst_ref=dst,
        send_sem=send_sem,
        recv_sem=recv_sem,
        device_id={axis: peer},
        device_id_type=MESH,
    )
    copy.start()
    return copy


def greet_all(with_head):
    me = lax.axis_index("seq")
    barrier = pltpu.get_barrier_semaphore()
    for step in range(1, NSEQ):
        pl.semaphore_signal(
            barrier, inc=1, device_id={"seq": (me + step) % NSEQ}, device_id_type=MESH
        )
    if with_head:
        other = 1 - lax.axis_index("head")
        pl.semaphore_signal(barrier, inc=1, device_id={"head": other}, device_id_type=MESH)
    pl.semaphore_wait(barrier, NSEQ - 1 + int(with_head))


def row_to_column(row):
    width = row.shape[1]
    same = lax.broadcasted_iota(jnp.int32, (width, width), 0) == lax.broadcasted_iota(
        jnp.int32, (width, width), 1
    )
    return jnp.sum(jnp.where(same, row, 0.0), axis=1, keepdims=True)


def start_stats(values, stats, send_sem, recv_sem):
    me = lax.axis_index("seq")
    ones = jnp.ones((8, values.shape[1]), jnp.float32)
    contract = (((1,), (1,)), ((), ()))
    for n, terms in enumerate((values, values * values)):
        stats[me, n : n + 1, :] = lax.dot_general(
            ones, terms, contract, precision=highest, preferred_element_type=jnp.float32
        )[0:1]
    return [
        send(
            stats.at[me],
            stats.at[me],
            send_sem.at[step - 1],
            recv_sem.at[step - 1],
            (me + step) % NSEQ,
        )
        for step in range(1, NSEQ)
    ]


def finish_stats(copies, stats):
    for copy in copies:
        copy.wait_recv()
    total = stats[0]
    for source in range(1, NSEQ):
        total = total + stats[source]
    mean = total[0:1, :] / D
    variance = total[1:2, :] / D - mean * mean
    return row_to_column(mean), row_to_column(lax.rsqrt(variance + eps_norm))


def add_into(target, extra):
    target[...] = (target[...].astype(jnp.float32) + extra[...].astype(jnp.float32)).astype(
        jnp.bfloat16
    )


class ReduceScatter:
    def __init__(self, parts, from_core, from_y, from_z, send_sem, recv_sem, produce):
        self.refs = parts, from_core, from_y, from_z
        self.sems = send_sem, recv_sem
        self.produce = produce
        me, z, y, c = place()
        self.turns = [(z + 1 + turn) % NZ for turn in range(NZ)]
        self.first, self.second, self.third = [], [], []

    def put(self, src, dst, sem, peer):
        send_sem, recv_sem = self.sems
        return send(src, dst, send_sem.at[sem], recv_sem.at[sem], peer)

    def pass_core(self, turn):
        me, z, y, c = place()
        parts, from_core, from_y, from_z = self.refs
        to = self.turns[turn]
        self.produce(1 - c, to)
        self.first.append(
            self.put(parts.at[1 - c, to], from_core.at[to], turn, me + 1 - 2 * c)
        )

    def own(self):
        me, z, y, c = place()
        for to in self.turns:
            self.produce(c, to)

    def pass_y(self, turn):
        me, z, y, c = place()
        parts, from_core, from_y, from_z = self.refs
        to = self.turns[turn]
        self.first[turn].wait_recv()
        add_into(parts.at[c, to, 1 - y], from_core.at[to, 1 - y])
        self.second.append(
            self.put(parts.at[c, to, 1 - y], from_y.at[to], NZ + turn, me + 2 - 4 * y)
        )
        if turn < NZ - 1:
            add_into(parts.at[c, to, y], from_core.at[to, y])

    def pass_z(self, turn):
        me, z, y, c = place()
        parts, from_core, from_y, from_z = self.refs
        to = self.turns[turn]
        self.second[turn].wait_recv()
        add_into(parts.at[c, to, y], from_y.at[to])
        self.third.append(
            self.put(
                parts.at[c, to, y], from_z.at[turn], 2 * NZ + turn, to * 4 + y * 2 + c
            )
        )

    def collect(self):
        me, z, y, c = place()
        parts, from_core, from_y, from_z = self.refs
        self.second[NZ - 1].wait_recv()
        total = (
            parts[c, z, y].astype(jnp.float32)
            + from_core[z, y].astype(jnp.float32)
            + from_y[z].astype(jnp.float32)
        )
        for turn in range(NZ - 1):
            self.third[turn].wait_recv()
            total = total + from_z[turn].astype(jnp.float32)
        return total

    def run(self):
        for turn in range(NZ):
            self.pass_core(turn)
        self.own()
        for turn in range(NZ):
            self.pass_y(turn)
            if turn > 0:
                self.pass_z(turn - 1)
        return self.collect()

    def copies(self):
        return self.first + self.second + self.third


def all_gather(blocks, send_sem, recv_sem, consume):
    me, z, y, c = place()
    own = blocks.at[c, z, y]
    turns = [(z + NZ - turn) % NZ for turn in range(NZ)]
    along_z = [
        send(
            own,
            own,
            send_sem.at[turn - 1],
            recv_sem.at[turn - 1],
            ((z + turn) % NZ) * 4 + y * 2 + c,
        )
        for turn in range(1, NZ)
    ]
    along_y, across = [], []

    def pass_y(turn):
        block = blocks.at[c, turns[turn], y]
        sem = NZ - 1 + turn
        along_y.append(send(block, block, send_sem.at[sem], recv_sem.at[sem], me + 2 - 4 * y))

    def pass_core(turn):
        along_y[turn].wait_recv()
        block = blocks.at[c, turns[turn]]
        sem = 2 * NZ - 1 + turn
        across.append(send(block, block, send_sem.at[sem], recv_sem.at[sem], me + 1 - 2 * c))
        consume(c, turns[turn])

    pass_y(0)
    for turn in range(1, NZ):
        along_z[turn - 1].wait_recv()
        pass_y(turn)
        pass_core(turn - 1)
    pass_core(NZ - 1)
    for turn in range(NZ):
        across[turn].wait_recv()
        consume(1 - c, turns[turn])
    return along_z + along_y + across


def columns_of(core, to, y, width):
    return pl.ds(pl.multiple_of((to * 4 + y * 2 + core) * width, width), width)


PAGES_STEP = 8


def visit_pages(
    turn, owners, numbers, lengths, slopes, keys, values, out, q_rows, tops, totals, owned
):
    requests = lengths.shape[0]
    nheads = NSEQ
    page_len = keys.shape[1]
    root = 128 ** (-0.5)
    group = 4
    ngroups = nheads // group
    width = group * 128
    count = 2 * nheads

    spot = lax.broadcasted_iota(jnp.int32, (2 * group, width), 0)
    own_head = spot % group == lax.broadcasted_iota(jnp.int32, (2 * group, width), 1) // 128
    first_step = spot < group
    row = lax.broadcasted_iota(jnp.int32, (count, nheads), 0)
    row_head = row // (2 * group) * group + row % group
    slope = jnp.sum(
        jnp.where(
            row_head == lax.broadcasted_iota(jnp.int32, (count, nheads), 1), slopes[...], 0.0
        ),
        axis=1,
        keepdims=True,
    )
    step_row = lax.broadcasted_iota(jnp.int32, (count, page_len), 0) // group % 2
    offset = lax.broadcasted_iota(jnp.int32, (count, page_len), 1)
    lane = lax.broadcasted_iota(jnp.int32, (count, 128), 1)
    lane_step = lax.broadcasted_iota(jnp.int32, (count, 128), 0) // group % 2
    lane_one = lax.broadcasted_iota(jnp.int32, (1, 128), 1)
    top_rows = tops[...]
    sum_rows = totals[...]
    owner_row = owned[0:1, :]
    page_outs = []
    for slot in range(PAGES_STEP):
        page = turn * PAGES_STEP + slot
        owner = owners[page]
        safe = jnp.clip(owner, 0, requests - 1)
        left = lengths[safe] - numbers[page] * page_len
        q_first = q_rows[pl.ds(safe, 1), :]
        q_second = q_rows[pl.ds(safe + requests, 1), :]
        scores = []
        for g in range(ngroups):
            columns = slice(g * width, (g + 1) * width)
            spread = jnp.where(
                own_head, jnp.where(first_step, q_first[:, columns], q_second[:, columns]), 0.0
            ).astype(jnp.bfloat16)
            scores.append(
                lax.dot_general(
                    spread,
                    keys[page, :, columns],
                    (((1,), (1,)), ((), ())),
                    preferred_element_type=jnp.float32,
                )
            )
        distance = (left + step_row - offset).astype(jnp.float32)
        score = jnp.concatenate(scores, axis=0) * root - distance * slope
        valid = (offset < left) & (owner >= 0)
        masked = jnp.where(valid, score, floor_score)
        top = jnp.max(masked, axis=1, keepdims=True)
        expon = jnp.where(valid, jnp.exp(masked - top), 0.0)
        total = jnp.sum(expon, axis=1, keepdims=True)
        mixed = []
        for g in range(ngroups):
            product = jnp.dot(
                expon[g * 2 * group : (g + 1) * 2 * group].astype(jnp.bfloat16),
                values[page, :, g * width : (g + 1) * width],
                preferred_element_type=jnp.float32,
            )
            mixed.append(jnp.where(own_head, product, 0.0))
        mixed = jnp.concatenate(mixed, axis=1)
        page_outs.append(jnp.sum(mixed[:group], axis=0, keepdims=True))
        page_outs.append(jnp.sum(mixed[group:], axis=0, keepdims=True))
        here = lane == 2 * page + lane_step
        top_rows = jnp.where(here, top, top_rows)
        sum_rows = jnp.where(here, total, sum_rows)
        owner_row = jnp.where(lane_one // 2 == page, owner.astype(jnp.float32), owner_row)
    tops[...] = top_rows
    totals[...] = sum_rows
    owned[0:1, :] = owner_row
    stacked = jnp.concatenate(page_outs, axis=0).astype(jnp.bfloat16)
    first = pl.multiple_of(turn * 2 * PAGES_STEP, 2 * PAGES_STEP)
    for head in range(nheads):
        out[head, pl.ds(first, 2 * PAGES_STEP), :] = stacked[:, head * 128 : head * 128 + 128]


def write_marks(marks, tops, totals, owned):
    group = 4
    even = lax.broadcasted_iota(jnp.int32, (1, 128), 1) % 2 == 0
    for head in range(NSEQ):
        at = head // group * 2 * group + head % group
        for n, rows in enumerate((tops[...], totals[...])):
            marks[head, n : n + 1, :] = jnp.where(
                even, rows[at : at + 1], rows[at + group : at + group + 1]
            )
        marks[head, 2:3, :] = owned[0:1, :]
        marks[head, 3:4, :] = jnp.zeros((1, 128), jnp.float32)


def combine(qkv, slopes, page_out, marks):
    rows = qkv.shape[0]
    requests = rows // 2
    me = lax.axis_index("seq")
    joined = qkv[...].astype(jnp.float32)
    query, new_key, new_value = joined[:, :128], joined[:, 128:256], joined[:, 256:]
    slope = jnp.sum(
        jnp.where(lax.broadcasted_iota(jnp.int32, slopes.shape, 1) == me, slopes[...], 0.0),
        axis=1,
        keepdims=True,
    )
    root = 128 ** (-0.5)
    same = jnp.sum(query * new_key, axis=1, keepdims=True) * root
    key_before = jnp.concatenate([new_key[:requests], new_key[:requests]], axis=0)
    value_before = jnp.concatenate([new_value[:requests], new_value[:requests]], axis=0)
    later = lax.broadcasted_iota(jnp.int32, (rows, 1), 0) >= requests
    before = jnp.where(
        later, jnp.sum(query * key_before, axis=1, keepdims=True) * root - slope, floor_score
    )
    row_id = lax.broadcasted_iota(jnp.int32, (rows, 128), 0)
    lane_step = lax.broadcasted_iota(jnp.int32, (rows, 128), 1) % 2
    row_step = row_id // requests
    row_owner = (row_id % requests).astype(jnp.float32)

    def member(source):
        return (marks[source, 2:3, :] == row_owner) & (lane_step == row_step)

    best = jnp.full((rows, 128), floor_score, jnp.float32)
    for source in range(NSEQ):
        best = jnp.maximum(best, jnp.where(member(source), marks[source, 0:1, :], floor_score))
    top = jnp.maximum(jnp.max(best, axis=1, keepdims=True), jnp.maximum(same, before))
    e_same = jnp.exp(same - top)
    e_before = jnp.where(later, jnp.exp(before - top), 0.0)
    sums = jnp.zeros((rows, 128), jnp.float32)
    mixed = e_same.astype(jnp.bfloat16).astype(jnp.float32) * new_value + e_before.astype(
        jnp.bfloat16
    ).astype(jnp.float32) * value_before
    live = page_out.shape[1]
    for source in range(NSEQ):
        factor = jnp.where(member(source), jnp.exp(marks[source, 0:1, :] - top), 0.0)
        sums = sums + factor * marks[source, 1:2, :]
        mixed = mixed + jnp.dot(
            factor[:, :live].astype(jnp.bfloat16),
            page_out[source],
            preferred_element_type=jnp.float32,
        )
    total = jnp.sum(sums, axis=1, keepdims=True) + e_same + e_before
    return (mixed / total).astype(jnp.bfloat16)


def layer_kernel(
    owners,
    numbers,
    lengths,
    tokens,
    slopes,
    gain_one,
    gain,
    w_qkv_hbm,
    keys_hbm,
    values_hbm,
    w_out_hbm,
    w_up_hbm,
    w_down_hbm,
    result,
    w_qkv,
    keys,
    values,
    w_out,
    w_up,
    w_down,
    q_parts,
    q_core,
    q_y,
    q_z,
    kv_parts,
    kv_core,
    kv_y,
    kv_z,
    q_all,
    qkv,
    q_rows,
    tops,
    totals,
    owned,
    page_out,
    marks,
    got_out,
    got_marks,
    attended,
    pair_out,
    stats_one,
    stats,
    parts,
    from_core,
    from_y,
    from_z,
    hidden,
    ex_send,
    ex_recv,
    pair_send,
    pair_recv,
    stat_send,
    stat_recv,
    rs_send,
    rs_recv,
    ag_send,
    ag_recv,
    load_sem,
    page_sem,
):
    load_qkv = pltpu.make_async_copy(w_qkv_hbm, w_qkv, load_sem.at[3])
    load_qkv.start()
    npages = keys.shape[0]
    nturns = npages // PAGES_STEP
    page_loads = []
    for turn in range(nturns):
        some = pl.ds(turn * PAGES_STEP, PAGES_STEP)
        for n, (src, dst) in enumerate(((keys_hbm, keys), (values_hbm, values))):
            load = pltpu.make_async_copy(src.at[some], dst.at[some], page_sem.at[turn, n])
            load.start()
            page_loads.append(load)
    loads = [
        pltpu.make_async_copy(src, dst, load_sem.at[n])
        for n, (src, dst) in enumerate(
            ((w_out_hbm, w_out), (w_up_hbm, w_up), (w_down_hbm, w_down))
        )
    ]
    for load in loads:
        load.start()
    me, z, y, c = place()
    other = 1 - lax.axis_index("head")
    greet_all(True)
    token_float = tokens[...].astype(jnp.float32)
    copies = start_stats(token_float, stats_one, stat_send.at[0], stat_recv.at[0])
    mean, scale = finish_stats(copies, stats_one)
    normed_one = ((token_float - mean) * scale * gain_one[...]).astype(jnp.bfloat16)
    load_qkv.wait()

    def produce_q(core, to):
        for side in range(2):
            q_parts[core, to, side] = jnp.dot(
                normed_one,
                w_qkv[0, :, columns_of(core, to, side, 128)],
                preferred_element_type=jnp.float32,
            ).astype(jnp.bfloat16)

    def produce_kv(core, to):
        for side in range(2):
            columns = columns_of(core, to, side, 128)
            weight = jnp.concatenate([w_qkv[1, :, columns], w_qkv[2, :, columns]], axis=1)
            kv_parts[core, to, side] = jnp.dot(
                normed_one, weight, preferred_element_type=jnp.float32
            ).astype(jnp.bfloat16)

    q_sum = ReduceScatter(q_parts, q_core, q_y, q_z, rs_send.at[0], rs_recv.at[0], produce_q)
    kv_sum = ReduceScatter(
        kv_parts, kv_core, kv_y, kv_z, rs_send.at[1], rs_recv.at[1], produce_kv
    )
    query = q_sum.run().astype(jnp.bfloat16)
    q_all[c, z, y] = query
    qkv[:, :128] = query

    def consume_q(core, source):
        if len(kv_sum.first) < NZ:
            kv_sum.pass_core(len(kv_sum.first))
        for side in range(2):
            q_rows[:, columns_of(core, source, side, 128)] = q_all[core, source, side].astype(
                jnp.float32
            )

    copies += all_gather(q_all, ag_send.at[2], ag_recv.at[2], consume_q)
    kv_sum.own()
    for turn in range(NZ):
        kv_sum.pass_y(turn)
    tops[...] = jnp.zeros_like(tops)
    totals[...] = jnp.zeros_like(totals)
    owned[...] = jnp.full_like(owned, -1.0)

    def visit(turn, carry):
        visit_pages(
            turn, owners, numbers, lengths, slopes, keys, values, page_out, q_rows, tops, totals,
            owned,
        )
        return carry

    arrivals = []
    for half in range(2):
        for load in page_loads[half * nturns : (half + 1) * nturns]:
            load.wait()
        lax.fori_loop(half * nturns // 2, (half + 1) * nturns // 2, visit, 0)
        if half == 0:
            for turn in range(NZ - 1):
                kv_sum.pass_z(turn)
        else:
            write_marks(marks, tops, totals, owned)
        rows = pl.ds(half * npages, npages)
        for step in range(1, NSEQ):
            to = (me + step) % NSEQ
            n = 3 * (step - 1) + half
            arrivals.append(
                send(
                    page_out.at[to, rows],
                    got_out.at[me, rows],
                    ex_send.at[n],
                    ex_recv.at[n],
                    to,
                )
            )
            if half == 1:
                arrivals.append(
                    send(
                        marks.at[to], got_marks.at[me], ex_send.at[n + 1], ex_recv.at[n + 1], to
                    )
                )
    got_out[me] = page_out[me]
    got_marks[me] = marks[me]
    qkv[:, 128:] = kv_sum.collect().astype(jnp.bfloat16)
    copies += q_sum.copies() + kv_sum.copies() + arrivals
    for copy in arrivals:
        copy.wait_recv()
    attended[c, z, y] = combine(qkv, slopes, got_out, got_marks)
    contract = (((1,), (1,)), ((), ()))
    sums = [jnp.zeros(result.shape, jnp.float32), jnp.zeros(result.shape, jnp.float32)]
    loads[0].wait()

    def consume_attended(core, source):
        for side in range(2):
            sums[0] = sums[0] + lax.dot_general(
                attended[core, source, side],
                w_out[:, columns_of(core, source, side, 128)],
                contract,
                preferred_element_type=jnp.float32,
            )

    copies += all_gather(attended, ag_send.at[0], ag_recv.at[0], consume_attended)
    projected = sums[0].astype(jnp.bfloat16)
    pair_out[0, 0] = projected
    pair = send(
        pair_out.at[0, 0], pair_out.at[0, 1], pair_send.at[0], pair_recv.at[0], other, "head"
    )
    copies.append(pair)
    pair.wait_recv()
    hidden_in = (
        tokens[...].astype(jnp.float32) + (projected.astype(jnp.float32) + pair_out[0, 1].astype(jnp.float32))
    ).astype(jnp.bfloat16)
    hidden_float = hidden_in.astype(jnp.float32)
    stat_copies = start_stats(hidden_float, stats, stat_send.at[1], stat_recv.at[1])
    copies += stat_copies
    mean, scale = finish_stats(stat_copies, stats)
    normed = ((hidden_float - mean) * scale * gain[...]).astype(jnp.bfloat16)
    loads[1].wait()
    share = parts.shape[4]

    def produce(core, to):
        for side in range(2):
            parts[core, to, side] = jnp.dot(
                normed,
                w_up[:, columns_of(core, to, side, share)],
                preferred_element_type=jnp.float32,
            ).astype(jnp.bfloat16)

    def consume_hidden(core, source):
        for side in range(2):
            sums[1] = sums[1] + lax.dot_general(
                hidden[core, source, side],
                w_down[:, columns_of(core, source, side, share)],
                contract,
                preferred_element_type=jnp.float32,
            )

    up_sum = ReduceScatter(
        parts, from_core, from_y, from_z, rs_send.at[2], rs_recv.at[2], produce
    )
    total = up_sum.run()
    copies += up_sum.copies()
    hidden[c, z, y] = (0.5 * total * (1.0 + lax.erf(total * 0.5**0.5))).astype(jnp.bfloat16)
    loads[2].wait()
    copies += all_gather(hidden, ag_send.at[1], ag_recv.at[1], consume_hidden)
    down = sums[1].astype(jnp.bfloat16)
    pair_out[1, 0] = down
    pair = send(
        pair_out.at[1, 0], pair_out.at[1, 1], pair_send.at[1], pair_recv.at[1], other, "head"
    )
    copies.append(pair)
    pair.wait_recv()
    result[...] = (hidden_float + (down.astype(jnp.float32) + pair_out[1, 1].astype(jnp.float32))).astype(jnp.bfloat16)
    for copy in copies:
        copy.wait_send()


def on_device_kernel(
    tokens,
    lengths,
    page_owner,
    page_number,
    key_pages,
    value_pages,
    alibi_slopes,
    norm1_gain,
    norm2_gain,
    w_qkv,
    w_out,
    w_up,
    w_down,
):
    nsteps, requests, local_width = tokens.shape
    rows = nsteps * requests
    npages = key_pages.shape[0]
    share = w_up.shape[1] // NSEQ
    by_input = jnp.transpose(w_qkv, (1, 0, 2))
    vmem = pl.BlockSpec(memory_space=pltpu.VMEM)
    smem = pl.BlockSpec(memory_space=pltpu.SMEM)
    hbm = pl.BlockSpec(memory_space=pl.ANY)
    dma = pltpu.SemaphoreType.DMA
    bf16 = jnp.bfloat16
    f32 = jnp.float32

    def sums(width):
        return [
            pltpu.VMEM((2, NZ, 2, rows, width), bf16),
            pltpu.VMEM((NZ, 2, rows, width), bf16),
            pltpu.VMEM((NZ, rows, width), bf16),
            pltpu.VMEM((NZ - 1, rows, width), bf16),
        ]

    result = pl.pallas_call(
        layer_kernel,
        out_shape=jax.ShapeDtypeStruct((rows, local_width), bf16),
        in_specs=[smem] * 3 + [vmem] * 4 + [hbm] * 6,
        out_specs=vmem,
        scratch_shapes=[
            pltpu.VMEM(by_input.shape, bf16),
            pltpu.VMEM(key_pages.shape, bf16),
            pltpu.VMEM(value_pages.shape, bf16),
            pltpu.VMEM(w_out.shape, bf16),
            pltpu.VMEM(w_up.shape, bf16),
            pltpu.VMEM(w_down.shape, bf16),
            *sums(128),
            *sums(256),
            pltpu.VMEM((2, NZ, 2, rows, 128), bf16),
            pltpu.VMEM((rows, 384), bf16),
            pltpu.VMEM((rows, NSEQ * 128), f32),
            pltpu.VMEM((2 * NSEQ, 128), f32),
            pltpu.VMEM((2 * NSEQ, 128), f32),
            pltpu.VMEM((8, 128), f32),
            pltpu.VMEM((NSEQ, 2 * npages, 128), bf16),
            pltpu.VMEM((NSEQ, 4, 128), f32),
            pltpu.VMEM((NSEQ, 2 * npages, 128), bf16),
            pltpu.VMEM((NSEQ, 4, 128), f32),
            pltpu.VMEM((2, NZ, 2, rows, 128), bf16),
            pltpu.VMEM((2, 2, rows, local_width), bf16),
            pltpu.VMEM((NSEQ, 2, rows), f32),
            pltpu.VMEM((NSEQ, 2, rows), f32),
            *sums(share),
            pltpu.VMEM((2, NZ, 2, rows, share), bf16),
            dma((3 * NSEQ - 3,)),
            dma((3 * NSEQ - 3,)),
            dma((2,)),
            dma((2,)),
            dma((2, NSEQ - 1)),
            dma((2, NSEQ - 1)),
            dma((3, COPIES)),
            dma((3, COPIES)),
            dma((3, COPIES)),
            dma((3, COPIES)),
            dma((4,)),
            dma((npages // PAGES_STEP, 2)),
        ],
        compiler_params=pltpu.CompilerParams(
            collective_id=0, has_side_effects=True, vmem_limit_bytes=VMEM_LIMIT
        ),
        name="layer",
    )(
        page_owner,
        page_number,
        lengths,
        tokens.reshape(rows, local_width),
        alibi_slopes[None, :],
        norm1_gain[None, :],
        norm2_gain[None, :],
        by_input,
        key_pages,
        value_pages,
        w_out,
        w_up,
        w_down,
    )
    return result.reshape(tokens.shape)


def solution(mesh):
    placed = (
        P(None, None, "seq"),
        P(),
        P("seq"),
        P("seq"),
        P("seq", None, "head"),
        P("seq", None, "head"),
        P("head"),
        P("seq"),
        P("seq"),
        P("seq", None, "head"),
        P("seq", "head"),
        P("seq", "head"),
        P("seq", "head"),
    )
    fits = mesh.shape["seq"] == NSEQ and mesh.shape["head"] == 2
    return jax.shard_map(
        on_device_kernel if fits else on_device, mesh=mesh, in_specs=placed, out_specs=P(None, None, "seq"), check_vma=False
    )
```
